128 devices in a mesh: dp: 2 (over core), context: 8 (over y, z_lo), tensor: 8 (over x, z_hi).
Axes of the slice: x: 4, y: 4, z: 4 (z_hi: 2, z_lo: 2; z = z_hi * 2 + z_lo), core: 2. Of those that a mesh axis runs over, the one named last changes fastest.
Arguments:
- queries: bfloat16 [32768, 8192], P(('dp', 'context', 'tensor')), parts along dimension 0, may hold values from -5 to 5
- rotated_key_rows: bfloat16 [32768, 1024], P(('dp', 'context', 'tensor')), parts along dimension 0, may hold values from -5 to 5
- stored_value_rows: bfloat16 [32768, 1024], P(('dp', 'context', 'tensor')), parts along dimension 0, may hold values from -5 to 5
- doc_lengths: int32 [32], P('dp'), parts along dimension 0, may hold values from 1 to 2048, 16384 in all
- block_order: int32 [128], P('dp'), parts along dimension 0, may hold values from 0 to 63, each once
Outputs:
- attended: bfloat16 [32768, 8192], P(('dp', 'context', 'tensor')), parts along dimension 0
The draws below stay inside these ranges and needn't reach their ends.
There are 2 independent parts, one for each index of `dp`. The reference program is written for one: setup_inputs(seed, part) draws one part's arguments, and reference() takes and returns one part's arrays. A program takes and returns all parts, laid end to end along the dimension named above; each array names one. Nothing has to cross between parts.
Inputs may be any that keep to these rules, and one draw needn't show every extreme that they name: `doc_lengths`: the 16 lengths sum to 16384; the longest is exactly 2048. `block_order`: A permutation of the 64 sequence blocks of 256 tokens.
All inputs are finite; a program needn't handle non-finite values.
Results may differ from the reference program's by a relative error of at most 0.0045.
Values may be sent and summed in bfloat16 or wider, within the bound.
No kernel may reach another device: no remote copies, remote signals or barrier semaphores. Data moves between devices by JAX's collectives and lax.ppermute only.
A program may use at most 128 MiB of HBM per device.

```python
import math
import jax
import jax.numpy as jnp
import numpy as np
from jax import lax

QUERY_HEADS = 64
KEY_VALUE_HEADS = 8
HEAD_SIZE = 128
NDOCS = 16
PACKED_TOKENS = 16384
NBLK = 64
MOSTDOC = 2048


def draw_rotated_key_rows(key, part):
    key = jax.random.fold_in(key, 7)
    attention_output = jnp.clip(jax.random.normal(key, (PACKED_TOKENS, KEY_VALUE_HEADS * HEAD_SIZE), jnp.float32), -5.0, 5.0)
    return attention_output.astype(jnp.bfloat16)


def draw_queries(key, part):
    key = jax.random.fold_in(key, 9)
    attention_output = jnp.clip(jax.random.normal(key, (PACKED_TOKENS, QUERY_HEADS * HEAD_SIZE), jnp.float32), -5.0, 5.0)
    return attention_output.astype(jnp.bfloat16)


def block_scale(rng, extent, pieces, smallest, high):
    factor_of = 1.0
    for axis_at, blocks in pieces:
        steps = jax.random.uniform(jax.random.fold_in(jax.random.fold_in(rng, 6), axis_at), (blocks,), jnp.float32, smallest / len(pieces), high / len(pieces))
        factor_of = factor_of * jnp.repeat(jnp.exp(steps), extent[axis_at] // blocks).reshape((-1,) + (1,) * (len(extent) - 1 - axis_at))
    return factor_of


def length_profile(count, total, limit, lean):
    loads = [(1 << 20) // math.isqrt(standing ** lean) + 1 for standing in range(2, count + 1)]
    spare, given = total - limit - (count - 1), [1] * (count - 1)
    while spare > 0:
        movable = [i for i in range(count - 1) if given[i] < limit]
        mass, remaining = sum([loads[i] for i in movable]), spare
        for i in movable:
            addition = min(limit - given[i], max(1, remaining * loads[i] // mass), spare)
            given[i] = given[i] + addition
            spare = spare - addition
    return np.array([limit] + given)


def uneven_parts(rng, count, total, most, lean):
    if count == 2:
        one = jax.random.randint(rng, (), max(1, total - most), min(most, total - 1) + 1)
        return jnp.stack([one, total - one])
    tallies = jnp.asarray(length_profile(count, total, most, lean), jnp.int32)
    pairs = (count - 1) // 2
    donor, sink = tallies[1:1 + 2 * pairs:2], tallies[2:2 + 2 * pairs:2]
    margin = jnp.minimum(donor - 1, most - sink)
    moved = jax.random.randint(jax.random.fold_in(rng, 1), (pairs,), 0, 1 << 20) % (margin + 1)
    tallies = tallies.at[1:1 + 2 * pairs:2].set(donor - moved).at[2:2 + 2 * pairs:2].set(sink + moved)
    return tallies[jax.random.permutation(jax.random.fold_in(rng, 2), count)]


def noise(key, dims, spread, reach, cuts=(), kind=jnp.bfloat16):
    level = block_scale(key, dims, cuts, -0.22, 0.18) if cuts else 1.0
    array = jax.random.normal(key, dims, jnp.float32) * spread * level
    return jnp.minimum(jnp.maximum(array, -reach), reach).astype(kind)


def setup_inputs(seed: int = 0, part: int = 0) -> dict:
    keys = jax.random.split(jax.random.key(seed), 6)
    own_keys = jax.random.split(jax.random.fold_in(keys[5], part), 6)
    return {
        "queries": draw_queries(jax.random.fold_in(jax.random.fold_in(keys[5], part), 71), part),
        "rotated_key_rows": draw_rotated_key_rows(jax.random.fold_in(jax.random.fold_in(keys[5], part), 71), part),
        "stored_value_rows": noise(own_keys[2], (PACKED_TOKENS, KEY_VALUE_HEADS * HEAD_SIZE), 1.0, 5.0, ((0, 64),)),
        "doc_lengths": uneven_parts(own_keys[3], NDOCS, PACKED_TOKENS, MOSTDOC, 2).astype(jnp.int32),
        "block_order": jax.random.permutation(own_keys[4], NBLK).astype(jnp.int32),
    }


def reference(queries, rotated_key_rows, stored_value_rows, doc_lengths, block_order):
    sequence_length = queries.shape[0]
    count_of_blocks = block_order.shape[0]
    block_length = sequence_length // count_of_blocks
    query_group_width = QUERY_HEADS // KEY_VALUE_HEADS
    places = jnp.arange(sequence_length, dtype=jnp.int32)
    doc_ends = jnp.cumsum(doc_lengths).astype(jnp.int32)
    doc_ids = lax.optimization_barrier(jnp.sum((places[:, None] >= doc_ends[None, :]).astype(jnp.int32), axis=1)).astype(jnp.int32)
    block_places = jnp.arange(count_of_blocks, dtype=jnp.int32)
    matches = (block_order[None, :] == block_places[:, None]).astype(jnp.int32)
    inverse_permutation = lax.optimization_barrier(jnp.sum(matches * block_places[None, :], axis=1)).astype(jnp.int32)
    query_sequence = jnp.take(queries.reshape(count_of_blocks, block_length, QUERY_HEADS * HEAD_SIZE), inverse_permutation, axis=0).reshape(sequence_length, KEY_VALUE_HEADS, query_group_width, HEAD_SIZE)
    key_sequence = jnp.take(rotated_key_rows.reshape(count_of_blocks, block_length, KEY_VALUE_HEADS * HEAD_SIZE), inverse_permutation, axis=0).reshape(sequence_length, KEY_VALUE_HEADS, HEAD_SIZE)
    value_sequence = jnp.take(stored_value_rows.reshape(count_of_blocks, block_length, KEY_VALUE_HEADS * HEAD_SIZE), inverse_permutation, axis=0).reshape(sequence_length, KEY_VALUE_HEADS, HEAD_SIZE)
    window_extent = MOSTDOC
    tile_len = min(512, sequence_length)
    padded_keys = jnp.concatenate([jnp.zeros((window_extent, KEY_VALUE_HEADS, HEAD_SIZE), jnp.bfloat16), key_sequence], axis=0)
    padded_values = jnp.concatenate([jnp.zeros((window_extent, KEY_VALUE_HEADS, HEAD_SIZE), jnp.bfloat16), value_sequence], axis=0)
    doc_padded = jnp.concatenate([jnp.full((window_extent,), -1, jnp.int32), doc_ids], axis=0)
    score_scale = 1.0 / math.sqrt(HEAD_SIZE)

    def one_tile(start):
        q_tile = lax.dynamic_slice_in_dim(query_sequence, start, tile_len)
        k_tile = lax.dynamic_slice_in_dim(padded_keys, start, window_extent + tile_len)
        v_tile = lax.dynamic_slice_in_dim(padded_values, start, window_extent + tile_len)
        k_doc = lax.dynamic_slice_in_dim(doc_padded, start, window_extent + tile_len)
        q_doc = lax.dynamic_slice_in_dim(doc_ids, start, tile_len)
        q_pos = start + jnp.arange(tile_len, dtype=jnp.int32)
        k_pos = start - window_extent + jnp.arange(window_extent + tile_len, dtype=jnp.int32)
        visible = (k_pos[None, :] <= q_pos[:, None]) & (k_doc[None, :] == q_doc[:, None])
        scores = jnp.einsum('rkgd,skd->kgrs', q_tile.astype(jnp.float32), k_tile.astype(jnp.float32)) * score_scale
        scores = jnp.where(visible, scores, -jnp.inf)
        row_peak = lax.optimization_barrier(jnp.max(scores, axis=-1))
        weights = jnp.exp(scores - row_peak[..., None])
        denom = lax.optimization_barrier(jnp.sum(weights, axis=-1))
        rounded = lax.optimization_barrier(weights.astype(jnp.bfloat16))
        mixed = jnp.einsum('kgrs,skd->kgrd', rounded.astype(jnp.float32), v_tile.astype(jnp.float32))
        attention_output = mixed / denom[..., None]
        return jnp.transpose(attention_output, (2, 0, 1, 3)).reshape(tile_len, QUERY_HEADS * HEAD_SIZE).astype(jnp.bfloat16)
    starts = jnp.arange(sequence_length // tile_len, dtype=jnp.int32) * tile_len
    out_seq = lax.map(one_tile, starts).reshape(count_of_blocks, block_length, QUERY_HEADS * HEAD_SIZE)
    return jnp.take(out_seq, block_order, axis=0).reshape(sequence_length, QUERY_HEADS * HEAD_SIZE)
```

```python
import functools
import math

import jax
import jax.numpy as jnp
from jax import lax
from jax.experimental import pallas as pl
from jax.experimental.pallas import tpu as pltpu
from jax.sharding import PartitionSpec as P

HEAD = 128
GROUP = 8
KV_HEADS = 8
DOCS = 16
HIDDEN = -1e30
CHUNKS = 4


def gather_kernel(past, order_ref, recv_ref, out_ref, inverse):
    blocks = order_ref.shape[0]

    def note(j, carry):
        inverse[order_ref[j]] = j
        return carry

    lax.fori_loop(0, blocks, note, 0)

    def fill(d, carry):
        s = order_ref[d]
        for u in range(past // 2):
            a = recv_ref[inverse[jnp.maximum(s - 1 - 2 * u, 0)], 0].astype(jnp.float32)
            b = recv_ref[inverse[jnp.maximum(s - 2 - 2 * u, 0)], 0].astype(jnp.float32)
            out_ref[d, u, 0] = jnp.concatenate([a[:8], b[:8]], axis=0).astype(jnp.bfloat16)
            out_ref[d, u, 1] = jnp.concatenate([a[8:], b[8:]], axis=0).astype(jnp.bfloat16)
        return carry

    lax.fori_loop(0, blocks, fill, 0)


def gather_windows(chunk, past, block_order, recv):
    blocks = block_order.shape[0]
    return pl.pallas_call(
        functools.partial(gather_kernel, past),
        out_shape=jax.ShapeDtypeStruct((blocks, past // 2, 2, 16, HEAD), jnp.bfloat16),
        grid_spec=pltpu.PrefetchScalarGridSpec(
            num_scalar_prefetch=1,
            grid=(1,),
            in_specs=[pl.BlockSpec((blocks, 1, 16, HEAD), lambda i, o: (0, chunk, 0, 0))],
            out_specs=pl.BlockSpec((blocks, past // 2, 2, 16, HEAD), lambda i, o: (0, 0, 0, 0, 0)),
            scratch_shapes=[pltpu.SMEM((blocks,), jnp.int32)],
        ),
        compiler_params=pltpu.CompilerParams(vmem_limit_bytes=24 << 20),
        cost_estimate=pl.CostEstimate(flops=0, bytes_accessed=3 << 20, transcendentals=0),
        name="gather_windows",
    )(block_order, recv)


def attend_kernel(q_ref, k_own, v_own, window, q_doc, k_doc, *rest):
    out_ref, keys, values = rest[-3:]
    rows = q_ref.shape[0]
    past_keys = keys.shape[0] - rows
    keys[:past_keys, :HEAD] = window[:, :, 0].reshape(past_keys, HEAD)
    keys[past_keys:, :HEAD] = k_own[...]
    keys[:, HEAD:] = k_doc[...]
    values[:past_keys, :HEAD] = window[:, :, 1].reshape(past_keys, HEAD)
    values[past_keys:, :HEAD] = v_own[...]
    values[:, HEAD:] = jnp.ones((past_keys + rows, HEAD), jnp.bfloat16)
    scale = math.log2(math.e) / math.sqrt(HEAD)
    causal = lax.broadcasted_iota(jnp.int32, (rows, rows), 0) >= lax.broadcasted_iota(
        jnp.int32, (rows, rows), 1
    )

    def one_head(g, carry):
        columns = pl.ds(pl.multiple_of(g * HEAD, HEAD), HEAD)
        q = jnp.concatenate([q_ref[:, columns], q_doc[...]], axis=1)
        dims = (((1,), (1,)), ((), ()))
        before = lax.dot_general(
            q, keys[:past_keys, :], dims, preferred_element_type=jnp.float32
        )
        own = lax.dot_general(q, keys[past_keys:, :], dims, preferred_element_type=jnp.float32)
        own = jnp.where(causal, own, HIDDEN)
        peak = jnp.maximum(
            jnp.max(before, axis=1, keepdims=True), jnp.max(own, axis=1, keepdims=True)
        )
        w_before = jnp.exp2((before - peak) * scale).astype(jnp.bfloat16)
        w_own = jnp.exp2((own - peak) * scale).astype(jnp.bfloat16)
        total = jnp.dot(w_before, values[:past_keys, :], preferred_element_type=jnp.float32)
        total += jnp.dot(w_own, values[past_keys:, :], preferred_element_type=jnp.float32)
        out_ref[:, columns] = (total[:, :HEAD] / total[:, HEAD:]).astype(jnp.bfloat16)
        return carry

    lax.fori_loop(0, GROUP, one_head, 0)


def attend(chunk, queries, own_keys, own_values, window, q_doc, k_doc, attended):
    rows, width = queries.shape
    halves = KV_HEADS // CHUNKS
    sources, pairs = window.shape[:2]
    per_half = sources // halves
    total_keys = per_half * pairs * 16 + rows
    head = lambda i: (0, CHUNKS * i + chunk)
    whole = lambda i: (0, 0)
    in_specs = [
        pl.BlockSpec((rows, GROUP * HEAD), head),
        pl.BlockSpec((rows, HEAD), head),
        pl.BlockSpec((rows, HEAD), head),
        pl.BlockSpec((per_half, pairs, 2, 16, HEAD), lambda i: (i, 0, 0, 0, 0)),
        pl.BlockSpec((rows, HEAD), whole),
        pl.BlockSpec((total_keys, HEAD), whole),
    ]
    operands = [queries, own_keys, own_values, window, q_doc, k_doc]
    aliases = {}
    if attended is not None:
        in_specs.append(pl.BlockSpec(memory_space=pl.ANY))
        operands.append(attended)
        aliases = {6: 0}
    pairs_done = halves * GROUP * rows * total_keys
    return pl.pallas_call(
        attend_kernel,
        out_shape=jax.ShapeDtypeStruct((rows, width), jnp.bfloat16),
        grid=(halves,),
        in_specs=in_specs,
        out_specs=pl.BlockSpec((rows, GROUP * HEAD), head),
        scratch_shapes=[
            pltpu.VMEM((total_keys, 2 * HEAD), jnp.bfloat16),
            pltpu.VMEM((total_keys, 2 * HEAD), jnp.bfloat16),
        ],
        input_output_aliases=aliases,
        compiler_params=pltpu.CompilerParams(vmem_limit_bytes=40 << 20),
        cost_estimate=pl.CostEstimate(
            flops=pairs_done * 2 * 4 * HEAD, bytes_accessed=5 << 20, transcendentals=pairs_done
        ),
        name="attend",
    )(*operands)


def body(queries, rotated_key_rows, stored_value_rows, doc_lengths, block_order):
    rows = queries.shape[0]
    axes = ("context", "tensor")
    blocks = block_order.shape[0]
    halves = KV_HEADS // CHUNKS
    groups = blocks // halves
    thin = rows // groups
    past = 8

    def sliced(x):
        x = x.reshape(groups, thin, halves, CHUNKS, HEAD).transpose(2, 0, 3, 1, 4)
        return x.reshape(blocks, CHUNKS, thin, HEAD)

    pieces = jnp.concatenate([sliced(rotated_key_rows), sliced(stored_value_rows)], axis=2)
    recv = lax.all_to_all(pieces, axes, split_axis=0, concat_axis=0, tiled=True)

    me = lax.axis_index("context") * lax.axis_size("tensor") + lax.axis_index("tensor")
    place = block_order[me]
    ends = jnp.cumsum(doc_lengths)
    far = jnp.full((HEAD - DOCS,), 1 << 30, jnp.int32)
    end = jnp.concatenate([ends, far])[None, :]
    start = jnp.concatenate([ends - doc_lengths, far])[None, :]
    q_pos = (place * rows + jnp.arange(rows, dtype=jnp.int32))[:, None]
    q_doc = ((q_pos >= start) & (q_pos < end)).astype(jnp.bfloat16)
    key = jnp.arange(past * rows, dtype=jnp.int32)
    within = key % 16
    slot = 2 * (key // 16 % (past // 2)) + within // thin
    key_block = place - 1 - slot
    key_pos = key_block * rows + key // (16 * (past // 2)) * thin + within % thin
    key_pos = jnp.concatenate([jnp.where(key_block >= 0, key_pos, -1)[:, None], q_pos])
    k_doc = jnp.where((key_pos >= start) & (key_pos < end), 0.0, HIDDEN).astype(jnp.bfloat16)

    attended = None
    windows = []
    for chunk in range(CHUNKS):
        sends = gather_windows(chunk, past, block_order, recv)
        windows.append(lax.all_to_all(sends, axes, split_axis=0, concat_axis=0, tiled=True))
    for chunk in range(CHUNKS):
        attended = attend(
            chunk, queries, rotated_key_rows, stored_value_rows, windows[chunk], q_doc, k_doc, attended
        )
    return attended


def solution(mesh):
    rows = P(("dp", "context", "tensor"), None)
    return jax.shard_map(
        body,
        mesh=mesh,
        in_specs=(rows, rows, rows, P("dp"), P("dp")),
        out_specs=rows,
        check_vma=False,
    )
```

```python
import functools
import math

import jax
import jax.numpy as jnp
from jax import lax
from jax.experimental import pallas as pl
from jax.experimental.pallas import tpu as pltpu
from jax.sharding import PartitionSpec as P

HEAD = 128
GROUP = 8
KV_HEADS = 8
DOCS = 16
HIDDEN = -1e30
UNITS = 4
CHUNKS = ((0, 3), (3, 1))
STACK = 4


def pieces_kernel(k_ref, v_ref, out_ref):
    thin = out_ref.shape[2] // 2
    tall = 2 * thin
    groups = out_ref.shape[0] // 2

    def some_rows(r, carry):
        rows = pl.ds(pl.multiple_of(r * tall, tall), tall)
        for h in range(KV_HEADS):
            k = k_ref[rows, h * HEAD : (h + 1) * HEAD].astype(jnp.float32)
            v = v_ref[rows, h * HEAD : (h + 1) * HEAD].astype(jnp.float32)
            for half in range(2):
                part = slice(half * thin, (half + 1) * thin)
                both = jnp.concatenate([k[part], v[part]], axis=0).astype(jnp.bfloat16)
                out_ref[h // UNITS * groups + 2 * r + half, h % UNITS] = both
        return carry

    lax.fori_loop(0, k_ref.shape[0] // tall, some_rows, 0)


def cut_pieces(own_keys, own_values, blocks):
    rows = own_keys.shape[0]
    thin = rows * KV_HEADS // (UNITS * blocks)
    return pl.pallas_call(
        pieces_kernel,
        out_shape=jax.ShapeDtypeStruct((blocks, UNITS, 2 * thin, HEAD), jnp.bfloat16),
        compiler_params=pltpu.CompilerParams(vmem_limit_bytes=24 << 20),
        cost_estimate=pl.CostEstimate(flops=0, bytes_accessed=2 << 20, transcendentals=0),
        name="cut_pieces",
    )(own_keys, own_values)


def gather_kernel(past, order_ref, recv_ref, out_ref, inverse):
    blocks = order_ref.shape[0]
    together = 4

    @pl.when(pl.program_id(0) == 0)
    def _():
        for j in range(blocks):
            inverse[order_ref[j]] = j

    def fill(i, carry):
        for d in range(together):
            d = i * together + d
            s = order_ref[d]
            for u in range(past // 2):
                a = recv_ref[inverse[jnp.maximum(s - 1 - 2 * u, 0)], 0].astype(jnp.float32)
                b = recv_ref[inverse[jnp.maximum(s - 2 - 2 * u, 0)], 0].astype(jnp.float32)
                out_ref[d, 0, u, 0] = jnp.concatenate([a[:8], b[:8]], axis=0).astype(jnp.bfloat16)
                out_ref[d, 0, u, 1] = jnp.concatenate([a[8:], b[8:]], axis=0).astype(jnp.bfloat16)
        return carry

    lax.fori_loop(0, blocks // together, fill, 0)


def gather_windows(first, units, past, block_order, recv):
    blocks = block_order.shape[0]
    pairs = past // 2
    return pl.pallas_call(
        functools.partial(gather_kernel, past),
        out_shape=jax.ShapeDtypeStruct((blocks, units, pairs, 2, 16, HEAD), jnp.bfloat16),
        grid_spec=pltpu.PrefetchScalarGridSpec(
            num_scalar_prefetch=1,
            grid=(units,),
            in_specs=[pl.BlockSpec((blocks, 1, 16, HEAD), lambda i, o: (0, first + i, 0, 0))],
            out_specs=pl.BlockSpec(
                (blocks, 1, pairs, 2, 16, HEAD), lambda i, o: (0, i, 0, 0, 0, 0)
            ),
            scratch_shapes=[pltpu.SMEM((blocks,), jnp.int32)],
        ),
        compiler_params=pltpu.CompilerParams(vmem_limit_bytes=24 << 20),
        cost_estimate=pl.CostEstimate(flops=0, bytes_accessed=units << 21, transcendentals=0),
        name="gather_windows",
    )(block_order, recv)


def attend_kernel(q_ref, k_own, v_own, window, q_doc, k_doc, *rest):
    out_ref, keys, values, stacked, scores_a, scores_b, peak_a, peak_b = rest[-8:]
    rows = q_ref.shape[0]
    total_keys = keys.shape[0]
    past_keys = total_keys - rows
    tall = STACK * rows
    keys[:past_keys, :HEAD] = window[:, 0, :, 0].reshape(past_keys, HEAD)
    keys[past_keys:, :HEAD] = k_own[...]
    keys[:, HEAD:] = k_doc[...]
    values[:past_keys, :HEAD] = window[:, 0, :, 1].reshape(past_keys, HEAD)
    values[past_keys:, :HEAD] = v_own[...]
    values[:, HEAD:] = jnp.ones((total_keys, HEAD), jnp.bfloat16)
    for g in range(GROUP):
        stacked[g * rows : (g + 1) * rows, :HEAD] = q_ref[:, g * HEAD : (g + 1) * HEAD]
        stacked[g * rows : (g + 1) * rows, HEAD:] = q_doc[...]
    scale = math.log2(math.e) / math.sqrt(HEAD)
    tiles = [(t, t + rows) for t in range(0, total_keys, rows)]
    causal = lax.broadcasted_iota(jnp.int32, (tall, rows), 0) % rows >= lax.broadcasted_iota(
        jnp.int32, (tall, rows), 1
    )

    def score(g, scores, peak):
        q = stacked[g * tall : (g + 1) * tall, :]
        most = None
        for a, b in tiles:
            s = lax.dot_general(
                q, keys[a:b, :], (((1,), (1,)), ((), ())), preferred_element_type=jnp.float32
            )
            if a == past_keys:
                s = jnp.where(causal, s, HIDDEN)
            scores[:, a:b] = s
            for lane in range(0, rows, HEAD):
                part = s[:, lane : lane + HEAD]
                most = part if most is None else jnp.maximum(most, part)
        peak[...] = jnp.broadcast_to(jnp.max(most, axis=1, keepdims=True), (tall, HEAD))

    def mix(g, scores, peak):
        most = jnp.concatenate([peak[...]] * (rows // HEAD), axis=1)
        mixed = None
        for a, b in tiles:
            w = jnp.exp2((scores[:, a:b] - most) * scale).astype(jnp.bfloat16)
            part = jnp.dot(w, values[a:b, :], preferred_element_type=jnp.float32)
            mixed = part if mixed is None else mixed + part
        out = (mixed[:, :HEAD] / mixed[:, HEAD:]).astype(jnp.bfloat16)
        for h in range(STACK):
            at = (g * STACK + h) * HEAD
            out_ref[:, at : at + HEAD] = out[h * rows : (h + 1) * rows]

    buffers = ((scores_a, peak_a), (scores_b, peak_b))
    stacks = GROUP // STACK
    score(0, *buffers[0])
    for g in range(stacks):
        if g + 1 < stacks:
            score(g + 1, *buffers[(g + 1) % 2])
        mix(g, *buffers[g % 2])


def attend(first, units, queries, own_keys, own_values, window, q_doc, k_doc, attended):
    rows, width = queries.shape
    halves = KV_HEADS // UNITS
    sources, _, pairs = window.shape[:3]
    per_half = sources // halves
    total_keys = per_half * pairs * 16 + rows
    tall = STACK * rows
    head = lambda i, c: (0, UNITS * i + first + c)
    whole = lambda i, c: (0, 0)
    in_specs = [
        pl.BlockSpec((rows, GROUP * HEAD), head),
        pl.BlockSpec((rows, HEAD), head),
        pl.BlockSpec((rows, HEAD), head),
        pl.BlockSpec((per_half, 1, pairs, 2, 16, HEAD), lambda i, c: (i, c, 0, 0, 0, 0)),
        pl.BlockSpec((rows, HEAD), whole),
        pl.BlockSpec((total_keys, HEAD), whole),
    ]
    operands = [queries, own_keys, own_values, window, q_doc, k_doc]
    aliases = {}
    if attended is not None:
        in_specs.append(pl.BlockSpec(memory_space=pl.ANY))
        operands.append(attended)
        aliases = {6: 0}
    done = halves * units * GROUP * rows * total_keys
    return pl.pallas_call(
        attend_kernel,
        out_shape=jax.ShapeDtypeStruct((rows, width), jnp.bfloat16),
        grid=(halves, units),
        in_specs=in_specs,
        out_specs=pl.BlockSpec((rows, GROUP * HEAD), head),
        scratch_shapes=[
            pltpu.VMEM((total_keys, 2 * HEAD), jnp.bfloat16),
            pltpu.VMEM((total_keys, 2 * HEAD), jnp.bfloat16),
            pltpu.VMEM((GROUP * rows, 2 * HEAD), jnp.bfloat16),
            pltpu.VMEM((tall, total_keys), jnp.float32),
            pltpu.VMEM((tall, total_keys), jnp.float32),
            pltpu.VMEM((tall, HEAD), jnp.float32),
            pltpu.VMEM((tall, HEAD), jnp.float32),
        ],
        input_output_aliases=aliases,
        compiler_params=pltpu.CompilerParams(vmem_limit_bytes=44 << 20),
        cost_estimate=pl.CostEstimate(
            flops=done * 2 * 4 * HEAD, bytes_accessed=units * 4 << 20, transcendentals=done
        ),
        name="attend",
    )(*operands)


def body(queries, rotated_key_rows, stored_value_rows, doc_lengths, block_order):
    rows = queries.shape[0]
    axes = ("context", "tensor")
    blocks = block_order.shape[0]
    thin = rows * KV_HEADS // (UNITS * blocks)
    past = 8
    pieces = cut_pieces(rotated_key_rows, stored_value_rows, blocks)
    recv = lax.all_to_all(pieces, axes, split_axis=0, concat_axis=0, tiled=True)

    me = lax.axis_index("context") * lax.axis_size("tensor") + lax.axis_index("tensor")
    place = block_order[me]
    ends = jnp.cumsum(doc_lengths)
    far = jnp.full((HEAD - DOCS,), 1 << 30, jnp.int32)
    end = jnp.concatenate([ends, far])[None, :]
    start = jnp.concatenate([ends - doc_lengths, far])[None, :]
    q_pos = (place * rows + jnp.arange(rows, dtype=jnp.int32))[:, None]
    q_doc = ((q_pos >= start) & (q_pos < end)).astype(jnp.bfloat16)
    key = jnp.arange(past * rows, dtype=jnp.int32)
    within = key % 16
    slot = 2 * (key // 16 % (past // 2)) + within // thin
    key_block = place - 1 - slot
    key_pos = key_block * rows + key // (16 * (past // 2)) * thin + within % thin
    key_pos = jnp.concatenate([jnp.where(key_block >= 0, key_pos, -1)[:, None], q_pos])
    k_doc = jnp.where((key_pos >= start) & (key_pos < end), 0.0, HIDDEN).astype(jnp.bfloat16)

    attended = None
    for first, units in CHUNKS:
        sends = gather_windows(first, units, past, block_order, recv)
        window = lax.all_to_all(sends, axes, split_axis=0, concat_axis=0, tiled=True)
        attended = attend(
            first, units, queries, rotated_key_rows, stored_value_rows, window, q_doc, k_doc, attended
        )
    return attended


def solution(mesh):
    rows = P(("dp", "context", "tensor"), None)
    return jax.shard_map(
        body,
        mesh=mesh,
        in_specs=(rows, rows, rows, P("dp"), P("dp")),
        out_specs=rows,
        check_vma=False,
    )
```

```python
import functools
import math

import jax
import jax.numpy as jnp
from jax import lax
from jax.experimental import pallas as pl
from jax.experimental.pallas import tpu as pltpu
from jax.sharding import PartitionSpec as P

HEAD = 128
GROUP = 8
KV_HEADS = 8
DOCS = 16
HIDDEN = -1e30
UNITS = 4
CHUNKS = ((0, 3), (3, 1))
STACK = 4
VMEM = 60 << 20


def pieces_kernel(k_ref, v_ref, out_ref):
    thin = out_ref.shape[2] // 2
    tall = 2 * thin
    groups = out_ref.shape[0] // 2

    def some_rows(r, carry):
        rows = pl.ds(pl.multiple_of(r * tall, tall), tall)
        for h in range(KV_HEADS):
            k = k_ref[rows, h * HEAD : (h + 1) * HEAD].astype(jnp.float32)
            v = v_ref[rows, h * HEAD : (h + 1) * HEAD].astype(jnp.float32)
            for half in range(2):
                part = slice(half * thin, (half + 1) * thin)
                both = jnp.concatenate([k[part], v[part]], axis=0).astype(jnp.bfloat16)
                out_ref[h // UNITS * groups + 2 * r + half, h % UNITS] = both
        return carry

    lax.fori_loop(0, k_ref.shape[0] // tall, some_rows, 0)


def cut_pieces(own_keys, own_values, blocks):
    rows = own_keys.shape[0]
    thin = rows * KV_HEADS // (UNITS * blocks)
    return pl.pallas_call(
        pieces_kernel,
        out_shape=jax.ShapeDtypeStruct((blocks, UNITS, 2 * thin, HEAD), jnp.bfloat16),
        compiler_params=pltpu.CompilerParams(vmem_limit_bytes=VMEM),
        cost_estimate=pl.CostEstimate(flops=0, bytes_accessed=2 << 20, transcendentals=0),
        name="cut_pieces",
    )(own_keys, own_values)


def gather_kernel(past, order_ref, recv_ref, *rest):
    out_refs, inverse = rest[:-1], rest[-1]
    blocks = order_ref.shape[0]
    part = out_refs[0].shape[0]
    step = pl.program_id(0)

    @pl.when(step == 0)
    def _():
        for j in range(blocks):
            inverse[order_ref[j]] = j

    def fill(d, carry):
        s = order_ref[step * part + d]
        for u in range(past // 2):
            near = inverse[jnp.maximum(s - 1 - 2 * u, 0)]
            far = inverse[jnp.maximum(s - 2 - 2 * u, 0)]
            for (first, units), out_ref in zip(CHUNKS, out_refs):
                for c in range(units):
                    a = recv_ref[near, first + c].astype(jnp.float32)
                    b = recv_ref[far, first + c].astype(jnp.float32)
                    keys = jnp.concatenate([a[:8], b[:8]], axis=0)
                    values = jnp.concatenate([a[8:], b[8:]], axis=0)
                    out_ref[d, c, u, 0] = keys.astype(jnp.bfloat16)
                    out_ref[d, c, u, 1] = values.astype(jnp.bfloat16)
        return carry

    lax.fori_loop(0, part, fill, 0)


def gather_windows(past, block_order, recv):
    blocks = block_order.shape[0]
    pairs = past // 2
    part = blocks // 4
    shape = lambda rows, units: (rows, units, pairs, 2, 16, HEAD)
    return pl.pallas_call(
        functools.partial(gather_kernel, past),
        out_shape=[
            jax.ShapeDtypeStruct(shape(blocks, units), jnp.bfloat16) for _, units in CHUNKS
        ],
        grid_spec=pltpu.PrefetchScalarGridSpec(
            num_scalar_prefetch=1,
            grid=(blocks // part,),
            in_specs=[pl.BlockSpec((blocks, UNITS, 16, HEAD), lambda i, o: (0, 0, 0, 0))],
            out_specs=[
                pl.BlockSpec(shape(part, units), lambda i, o: (i, 0, 0, 0, 0, 0))
                for _, units in CHUNKS
            ],
            scratch_shapes=[pltpu.SMEM((blocks,), jnp.int32)],
        ),
        compiler_params=pltpu.CompilerParams(vmem_limit_bytes=VMEM),
        cost_estimate=pl.CostEstimate(flops=0, bytes_accessed=10 << 20, transcendentals=0),
        name="gather_windows",
    )(block_order, recv)


def attend_kernel(q_ref, k_own, v_own, window, q_doc, k_doc, *rest):
    out_ref, keys, values, stacked, scores_a, scores_b, peak_a, peak_b = rest[-8:]
    rows = q_ref.shape[0]
    total_keys = keys.shape[0]
    past_keys = total_keys - rows
    tall = STACK * rows
    keys[:past_keys, :HEAD] = window[:, 0, :, 0].reshape(past_keys, HEAD)
    keys[past_keys:, :HEAD] = k_own[...]
    keys[:, HEAD:] = k_doc[...]
    values[:past_keys, :HEAD] = window[:, 0, :, 1].reshape(past_keys, HEAD)
    values[past_keys:, :HEAD] = v_own[...]
    values[:, HEAD:] = jnp.ones((total_keys, HEAD), jnp.bfloat16)
    for g in range(GROUP):
        stacked[g * rows : (g + 1) * rows, :HEAD] = q_ref[:, g * HEAD : (g + 1) * HEAD]
        stacked[g * rows : (g + 1) * rows, HEAD:] = q_doc[...]
    scale = math.log2(math.e) / math.sqrt(HEAD)
    tiles = [(t, t + rows) for t in range(0, total_keys, rows)]
    causal = lax.broadcasted_iota(jnp.int32, (tall, rows), 0) % rows >= lax.broadcasted_iota(
        jnp.int32, (tall, rows), 1
    )

    def score(g, scores, peak):
        q = stacked[g * tall : (g + 1) * tall, :]
        most = None
        for a, b in tiles:
            s = lax.dot_general(
                q, keys[a:b, :], (((1,), (1,)), ((), ())), preferred_element_type=jnp.float32
            )
            if a == past_keys:
                s = jnp.where(causal, s, HIDDEN)
            scores[:, a:b] = s
            for lane in range(0, rows, HEAD):
                part = s[:, lane : lane + HEAD]
                most = part if most is None else jnp.maximum(most, part)
        peak[...] = jnp.broadcast_to(jnp.max(most, axis=1, keepdims=True), (tall, HEAD))

    def mix(g, scores, peak):
        most = jnp.concatenate([peak[...]] * (rows // HEAD), axis=1)
        mixed = None
        for a, b in tiles:
            w = jnp.exp2((scores[:, a:b] - most) * scale).astype(jnp.bfloat16)
            part = jnp.dot(w, values[a:b, :], preferred_element_type=jnp.float32)
            mixed = part if mixed is None else mixed + part
        out = (mixed[:, :HEAD] / mixed[:, HEAD:]).astype(jnp.bfloat16)
        for h in range(STACK):
            at = (g * STACK + h) * HEAD
            out_ref[:, at : at + HEAD] = out[h * rows : (h + 1) * rows]

    buffers = ((scores_a, peak_a), (scores_b, peak_b))
    stacks = GROUP // STACK
    score(0, *buffers[0])
    for g in range(stacks):
        if g + 1 < stacks:
            score(g + 1, *buffers[(g + 1) % 2])
        mix(g, *buffers[g % 2])


def attend(first, units, queries, own_keys, own_values, window, q_doc, k_doc, attended):
    rows, width = queries.shape
    halves = KV_HEADS // UNITS
    sources, _, pairs = window.shape[:3]
    per_half = sources // halves
    total_keys = per_half * pairs * 16 + rows
    tall = STACK * rows
    head = lambda i, c: (0, UNITS * i + first + c)
    whole = lambda i, c: (0, 0)
    in_specs = [
        pl.BlockSpec((rows, GROUP * HEAD), head),
        pl.BlockSpec((rows, HEAD), head),
        pl.BlockSpec((rows, HEAD), head),
        pl.BlockSpec((per_half, 1, pairs, 2, 16, HEAD), lambda i, c: (i, c, 0, 0, 0, 0)),
        pl.BlockSpec((rows, HEAD), whole),
        pl.BlockSpec((total_keys, HEAD), whole),
    ]
    operands = [queries, own_keys, own_values, window, q_doc, k_doc]
    aliases = {}
    if attended is not None:
        in_specs.append(pl.BlockSpec(memory_space=pl.ANY))
        operands.append(attended)
        aliases = {6: 0}
    done = halves * units * GROUP * rows * total_keys
    return pl.pallas_call(
        attend_kernel,
        out_shape=jax.ShapeDtypeStruct((rows, width), jnp.bfloat16),
        grid=(halves, units),
        in_specs=in_specs,
        out_specs=pl.BlockSpec((rows, GROUP * HEAD), head),
        scratch_shapes=[
            pltpu.VMEM((total_keys, 2 * HEAD), jnp.bfloat16),
            pltpu.VMEM((total_keys, 2 * HEAD), jnp.bfloat16),
            pltpu.VMEM((GROUP * rows, 2 * HEAD), jnp.bfloat16),
            pltpu.VMEM((tall, total_keys), jnp.float32),
            pltpu.VMEM((tall, total_keys), jnp.float32),
            pltpu.VMEM((tall, HEAD), jnp.float32),
            pltpu.VMEM((tall, HEAD), jnp.float32),
        ],
        input_output_aliases=aliases,
        compiler_params=pltpu.CompilerParams(vmem_limit_bytes=VMEM),
        cost_estimate=pl.CostEstimate(
            flops=done * 2 * 4 * HEAD, bytes_accessed=units * 4 << 20, transcendentals=done
        ),
        name="attend",
    )(*operands)


def body(queries, rotated_key_rows, stored_value_rows, doc_lengths, block_order):
    rows = queries.shape[0]
    axes = ("context", "tensor")
    blocks = block_order.shape[0]
    thin = rows * KV_HEADS // (UNITS * blocks)
    past = 8
    pieces = cut_pieces(rotated_key_rows, stored_value_rows, blocks)
    recv = lax.all_to_all(pieces, axes, split_axis=0, concat_axis=0, tiled=True)

    sends = gather_windows(past, block_order, recv)
    sends, own = lax.optimization_barrier((sends, (rotated_key_rows, stored_value_rows)))
    windows = [lax.all_to_all(sends[0], axes, split_axis=0, concat_axis=0, tiled=True)]
    windows[0], doc_lengths, block_order, rest = lax.optimization_barrier(
        (windows[0], doc_lengths, block_order, sends[1:])
    )
    for send in rest:
        windows.append(lax.all_to_all(send, axes, split_axis=0, concat_axis=0, tiled=True))

    me = lax.axis_index("context") * lax.axis_size("tensor") + lax.axis_index("tensor")
    place = block_order[me]
    ends = jnp.cumsum(doc_lengths)
    far = jnp.full((HEAD - DOCS,), 1 << 30, jnp.int32)
    end = jnp.concatenate([ends, far])[None, :]
    start = jnp.concatenate([ends - doc_lengths, far])[None, :]
    q_pos = (place * rows + jnp.arange(rows, dtype=jnp.int32))[:, None]
    q_doc = ((q_pos >= start) & (q_pos < end)).astype(jnp.bfloat16)
    key = jnp.arange(past * rows, dtype=jnp.int32)
    within = key % 16
    slot = 2 * (key // 16 % (past // 2)) + within // thin
    key_block = place - 1 - slot
    key_pos = key_block * rows + key // (16 * (past // 2)) * thin + within % thin
    key_pos = jnp.concatenate([jnp.where(key_block >= 0, key_pos, -1)[:, None], q_pos])
    k_doc = jnp.where((key_pos >= start) & (key_pos < end), 0.0, HIDDEN).astype(jnp.bfloat16)

    attended = None
    for (first, units), window in zip(CHUNKS, windows):
        attended = attend(first, units, queries, *own, window, q_doc, k_doc, attended)
    return attended


def solution(mesh):
    rows = P(("dp", "context", "tensor"), None)
    return jax.shard_map(
        body,
        mesh=mesh,
        in_specs=(rows, rows, rows, P("dp"), P("dp")),
        out_specs=rows,
        check_vma=False,
    )
```

```python
import functools
import math

import jax
import jax.numpy as jnp
from jax import lax
from jax.experimental import pallas as pl
from jax.experimental.pallas import tpu as pltpu
from jax.sharding import PartitionSpec as P

HEAD = 128
GROUP = 8
KV_HEADS = 8
HIDDEN = -1e30
UNITS = 4
CHUNKS = ((0, 3), (3, 1))
STACK = 4
VMEM = 62 << 20


def pieces_kernel(k_ref, v_ref, out_ref):
    thin = out_ref.shape[2] // 2
    tall = 2 * thin
    groups = out_ref.shape[0] // 2

    def some_rows(r, carry):
        rows = pl.ds(pl.multiple_of(r * tall, tall), tall)
        for h in range(KV_HEADS):
            k = k_ref[rows, h * HEAD : (h + 1) * HEAD].astype(jnp.float32)
            v = v_ref[rows, h * HEAD : (h + 1) * HEAD].astype(jnp.float32)
            for half in range(2):
                part = slice(half * thin, (half + 1) * thin)
                both = jnp.concatenate([k[part], v[part]], axis=0).astype(jnp.bfloat16)
                out_ref[h // UNITS * groups + 2 * r + half, h % UNITS] = both
        return carry

    lax.fori_loop(0, k_ref.shape[0] // tall, some_rows, 0)


def cut_pieces(own_keys, own_values, blocks):
    rows = own_keys.shape[0]
    thin = rows * KV_HEADS // (UNITS * blocks)
    return pl.pallas_call(
        pieces_kernel,
        out_shape=jax.ShapeDtypeStruct((blocks, UNITS, 2 * thin, HEAD), jnp.bfloat16),
        compiler_params=pltpu.CompilerParams(vmem_limit_bytes=VMEM),
        cost_estimate=pl.CostEstimate(flops=0, bytes_accessed=2 << 20, transcendentals=0),
        name="cut_pieces",
    )(own_keys, own_values)


def gather_kernel(past, order_ref, recv_ref, *rest):
    out_refs, inverse = rest[:-1], rest[-1]
    blocks = order_ref.shape[0]
    part = out_refs[0].shape[0]
    step = pl.program_id(0)

    @pl.when(step == 0)
    def _():
        for j in range(blocks):
            inverse[order_ref[j]] = j

    def fill(d, carry):
        s = order_ref[step * part + d]
        for u in range(past // 2):
            near = inverse[jnp.maximum(s - 1 - 2 * u, 0)]
            far = inverse[jnp.maximum(s - 2 - 2 * u, 0)]
            for (first, units), out_ref in zip(CHUNKS, out_refs):
                for c in range(units):
                    a = recv_ref[near, first + c].astype(jnp.float32)
                    b = recv_ref[far, first + c].astype(jnp.float32)
                    keys = jnp.concatenate([a[:8], b[:8]], axis=0)
                    values = jnp.concatenate([a[8:], b[8:]], axis=0)
                    out_ref[d, c, u, 0] = keys.astype(jnp.bfloat16)
                    out_ref[d, c, u, 1] = values.astype(jnp.bfloat16)
        return carry

    lax.fori_loop(0, part, fill, 0)


def gather_windows(past, block_order, recv):
    blocks = block_order.shape[0]
    pairs = past // 2
    part = blocks // 4
    shape = lambda rows, units: (rows, units, pairs, 2, 16, HEAD)
    return pl.pallas_call(
        functools.partial(gather_kernel, past),
        out_shape=[
            jax.ShapeDtypeStruct(shape(blocks, units), jnp.bfloat16) for _, units in CHUNKS
        ],
        grid_spec=pltpu.PrefetchScalarGridSpec(
            num_scalar_prefetch=1,
            grid=(blocks // part,),
            in_specs=[pl.BlockSpec((blocks, UNITS, 16, HEAD), lambda i, o: (0, 0, 0, 0))],
            out_specs=[
                pl.BlockSpec(shape(part, units), lambda i, o: (i, 0, 0, 0, 0, 0))
                for _, units in CHUNKS
            ],
            scratch_shapes=[pltpu.SMEM((blocks,), jnp.int32)],
        ),
        compiler_params=pltpu.CompilerParams(vmem_limit_bytes=VMEM),
        cost_estimate=pl.CostEstimate(flops=0, bytes_accessed=10 << 20, transcendentals=0),
        name="gather_windows",
    )(block_order, recv)


def mark_documents(lengths_ref, place, keys, stacked):
    total_keys, rows = keys.shape[0], stacked.shape[0] // GROUP
    lane = lax.broadcasted_iota(jnp.int32, (8, HEAD), 1)
    row = lax.broadcasted_iota(jnp.int32, (8, HEAD), 0)
    start = jnp.full((8, HEAD), 1 << 30, jnp.int32)
    end = start
    at = 0
    for d in range(lengths_ref.shape[0]):
        start = jnp.where(lane == d, at, start)
        at += lengths_ref[d]
        end = jnp.where(lane == d, at, end)

    def pair(base_a, base_b, inside, outside):
        both = [
            jnp.where((base + row >= start) & (base + row < end), inside, outside)
            for base in (base_a, base_b)
        ]
        return jnp.concatenate(both, axis=0).astype(jnp.bfloat16)

    past_keys = total_keys - rows
    slots = past_keys // rows

    def past(r, carry):
        for u in range(slots // 2):
            bases = []
            for slot in (2 * u, 2 * u + 1):
                block = place - 1 - slot
                bases.append(jnp.where(block >= 0, block * rows + r * 8, -8))
            to = pl.ds(pl.multiple_of((r * (slots // 2) + u) * 16, 16), 16)
            keys[to, HEAD:] = pair(*bases, 0.0, HIDDEN)
        return carry

    lax.fori_loop(0, rows // 8, past, 0)
    for r in range(rows // 16):
        base = place * rows + r * 16
        keys[past_keys + r * 16 : past_keys + r * 16 + 16, HEAD:] = pair(
            base, base + 8, 0.0, HIDDEN
        )
        marks = pair(base, base + 8, 1.0, 0.0)
        for g in range(GROUP):
            stacked[g * rows + r * 16 : g * rows + r * 16 + 16, HEAD:] = marks


def attend_kernel(lengths_ref, order_ref, me_ref, q_ref, k_own, v_own, window, *rest):
    out_ref, keys, values, stacked, scores_a, scores_b, peak_a, peak_b = rest[-8:]
    rows = q_ref.shape[0]
    total_keys = keys.shape[0]
    past_keys = total_keys - rows
    tall = STACK * rows

    @pl.when((pl.program_id(0) == 0) & (pl.program_id(1) == 0))
    def _():
        mark_documents(lengths_ref, order_ref[me_ref[0]], keys, stacked)
        values[:, HEAD:] = jnp.ones((total_keys, HEAD), jnp.bfloat16)

    keys[:past_keys, :HEAD] = window[:, 0, :, 0].reshape(past_keys, HEAD)
    keys[past_keys:, :HEAD] = k_own[...]
    values[:past_keys, :HEAD] = window[:, 0, :, 1].reshape(past_keys, HEAD)
    values[past_keys:, :HEAD] = v_own[...]
    for g in range(GROUP):
        stacked[g * rows : (g + 1) * rows, :HEAD] = q_ref[:, g * HEAD : (g + 1) * HEAD]
    scale = math.log2(math.e) / math.sqrt(HEAD)
    tiles = [(t, t + rows) for t in range(0, total_keys, rows)]
    causal = lax.broadcasted_iota(jnp.int32, (tall, rows), 0) % rows >= lax.broadcasted_iota(
        jnp.int32, (tall, rows), 1
    )

    def score(g, scores, peak):
        q = stacked[g * tall : (g + 1) * tall, :]
        most = None
        for a, b in tiles:
            s = lax.dot_general(
                q, keys[a:b, :], (((1,), (1,)), ((), ())), preferred_element_type=jnp.float32
            )
            if a == past_keys:
                s = jnp.where(causal, s, HIDDEN)
            scores[:, a:b] = s
            for lane in range(0, rows, HEAD):
                part = s[:, lane : lane + HEAD]
                most = part if most is None else jnp.maximum(most, part)
        peak[...] = jnp.broadcast_to(jnp.max(most, axis=1, keepdims=True), (tall, HEAD))

    def mix(g, scores, peak):
        most = jnp.concatenate([peak[...]] * (rows // HEAD), axis=1)
        mixed = None
        for a, b in tiles:
            w = jnp.exp2((scores[:, a:b] - most) * scale).astype(jnp.bfloat16)
            part = jnp.dot(w, values[a:b, :], preferred_element_type=jnp.float32)
            mixed = part if mixed is None else mixed + part
        out = (mixed[:, :HEAD] / mixed[:, HEAD:]).astype(jnp.bfloat16)
        for h in range(STACK):
            at = (g * STACK + h) * HEAD
            out_ref[:, at : at + HEAD] = out[h * rows : (h + 1) * rows]

    buffers = ((scores_a, peak_a), (scores_b, peak_b))
    stacks = GROUP // STACK
    score(0, *buffers[0])
    for g in range(stacks):
        if g + 1 < stacks:
            score(g + 1, *buffers[(g + 1) % 2])
        mix(g, *buffers[g % 2])


def attend(first, units, lengths, order, me, queries, own_keys, own_values, window, attended):
    rows, width = queries.shape
    halves = KV_HEADS // UNITS
    sources, _, pairs = window.shape[:3]
    per_half = sources // halves
    total_keys = per_half * pairs * 16 + rows
    tall = STACK * rows
    head = lambda i, c, *scalars: (0, UNITS * i + first + c)
    in_specs = [
        pl.BlockSpec((rows, GROUP * HEAD), head),
        pl.BlockSpec((rows, HEAD), head),
        pl.BlockSpec((rows, HEAD), head),
        pl.BlockSpec((per_half, 1, pairs, 2, 16, HEAD), lambda i, c, *scalars: (i, c, 0, 0, 0, 0)),
    ]
    operands = [lengths, order, me, queries, own_keys, own_values, window]
    aliases = {}
    if attended is not None:
        in_specs.append(pl.BlockSpec(memory_space=pl.ANY))
        aliases = {len(operands): 0}
        operands.append(attended)
    done = halves * units * GROUP * rows * total_keys
    return pl.pallas_call(
        attend_kernel,
        out_shape=jax.ShapeDtypeStruct((rows, width), jnp.bfloat16),
        grid_spec=pltpu.PrefetchScalarGridSpec(
            num_scalar_prefetch=3,
            grid=(halves, units),
            in_specs=in_specs,
            out_specs=pl.BlockSpec((rows, GROUP * HEAD), head),
            scratch_shapes=[
                pltpu.VMEM((total_keys, 2 * HEAD), jnp.bfloat16),
                pltpu.VMEM((total_keys, 2 * HEAD), jnp.bfloat16),
                pltpu.VMEM((GROUP * rows, 2 * HEAD), jnp.bfloat16),
                pltpu.VMEM((tall, total_keys), jnp.float32),
                pltpu.VMEM((tall, total_keys), jnp.float32),
                pltpu.VMEM((tall, HEAD), jnp.float32),
                pltpu.VMEM((tall, HEAD), jnp.float32),
            ],
        ),
        input_output_aliases=aliases,
        compiler_params=pltpu.CompilerParams(vmem_limit_bytes=VMEM),
        cost_estimate=pl.CostEstimate(
            flops=done * 2 * 4 * HEAD, bytes_accessed=units * 4 << 20, transcendentals=done
        ),
        name="attend",
    )(*operands)


def body(queries, rotated_key_rows, stored_value_rows, doc_lengths, block_order):
    axes = ("context", "tensor")
    blocks = block_order.shape[0]
    past = 8
    me = lax.axis_index("context") * lax.axis_size("tensor") + lax.axis_index("tensor")
    me = me.astype(jnp.int32).reshape(1)
    pieces = cut_pieces(rotated_key_rows, stored_value_rows, blocks)
    pieces, me = lax.optimization_barrier((pieces, me))
    recv = lax.all_to_all(pieces, axes, split_axis=0, concat_axis=0, tiled=True)
    sends = gather_windows(past, block_order, recv)
    sends, me = lax.optimization_barrier((sends, me))
    first = lax.all_to_all(sends[0], axes, split_axis=0, concat_axis=0, tiled=True)
    first, me, rest = lax.optimization_barrier((first, me, sends[1:]))
    windows = [first]
    for send in rest:
        windows.append(lax.all_to_all(send, axes, split_axis=0, concat_axis=0, tiled=True))
    attended = None
    own = (queries, rotated_key_rows, stored_value_rows)
    for (begin, units), window in zip(CHUNKS, windows):
        attended = attend(begin, units, doc_lengths, block_order, me, *own, window, attended)
    return attended


def solution(mesh):
    rows = P(("dp", "context", "tensor"), None)
    return jax.shard_map(
        body,
        mesh=mesh,
        in_specs=(rows, rows, rows, P("dp"), P("dp")),
        out_specs=rows,
        check_vma=False,
    )
```

```python
import functools
import math

import jax
import jax.numpy as jnp
from jax import lax
from jax.experimental import pallas as pl
from jax.experimental.pallas import tpu as pltpu
from jax.sharding import PartitionSpec as P

HEAD = 128
GROUP = 8
KV_HEADS = 8
HIDDEN = -1e30
CHUNKS = ((0, 5), (5, 2), (7, 1))
THIN = 4
STACK = 4
VMEM = 62 << 20


def pieces_kernel(k_ref, v_ref, out_ref):
    tall = 16
    lower = lax.broadcasted_iota(jnp.int32, (8, HEAD), 0) < THIN

    def some_rows(r, carry):
        rows = pl.ds(pl.multiple_of(r * tall, tall), tall)
        for pair in range(KV_HEADS // 2):
            halves = []
            for h in (2 * pair, 2 * pair + 1):
                k = k_ref[rows, h * HEAD : (h + 1) * HEAD].astype(jnp.float32)
                v = v_ref[rows, h * HEAD : (h + 1) * HEAD].astype(jnp.float32)
                parts = []
                for at in (0, 8):
                    k8, v8 = k[at : at + 8], v[at : at + 8]
                    parts.append(jnp.where(lower, k8, pltpu.roll(v8, THIN, 0)))
                    parts.append(jnp.where(lower, pltpu.roll(k8, THIN, 0), v8))
                halves.append(parts)
            for j in range(tall // THIN):
                both = jnp.concatenate([halves[0][j], halves[1][j]], axis=0)
                out_ref[r * (tall // THIN) + j, pair] = both.astype(jnp.bfloat16)
        return carry

    lax.fori_loop(0, k_ref.shape[0] // tall, some_rows, 0, unroll=2)


def cut_pieces(own_keys, own_values):
    blocks = own_keys.shape[0] // THIN
    return pl.pallas_call(
        pieces_kernel,
        out_shape=jax.ShapeDtypeStruct((blocks, KV_HEADS // 2, 16, HEAD), jnp.bfloat16),
        compiler_params=pltpu.CompilerParams(vmem_limit_bytes=VMEM),
        cost_estimate=pl.CostEstimate(flops=0, bytes_accessed=2 << 20, transcendentals=0),
        name="cut_pieces",
    )(own_keys, own_values)


def gather_kernel(past, order_ref, recv_ref, *rest):
    out_refs, (inverse, plain, rolled) = rest[:-3], rest[-3:]
    blocks = order_ref.shape[0]
    part = out_refs[0].shape[0]
    step = pl.program_id(0)
    lower = lax.broadcasted_iota(jnp.int32, (8, HEAD), 0) < THIN

    @pl.when(step == 0)
    def _():
        for j in range(blocks):
            inverse[order_ref[j]] = j

        def open_block(j, carry):
            for pair in range(KV_HEADS // 2):
                x = recv_ref[j, pair].astype(jnp.float32)
                for half in range(2):
                    h = 2 * pair + half
                    x8 = x[8 * half : 8 * half + 8]
                    plain[j, h] = x8
                    rolled[j, h] = pltpu.roll(x8, THIN, 0)
            return carry

        lax.fori_loop(0, blocks, open_block, 0, unroll=4)

    def fill(d, carry):
        s = order_ref[step * part + d]
        held = [inverse[jnp.maximum(s - 1 - slot, 0)] for slot in range(past)]
        for (first, units), out_ref in zip(CHUNKS, out_refs):
            for c in range(units):
                h = first + c
                for tile in range(past // 4):
                    keys, values = [], []
                    for slot in (4 * tile, 4 * tile + 2):
                        near, far = held[slot], held[slot + 1]
                        keys.append(jnp.where(lower, plain[near, h], rolled[far, h]))
                        values.append(jnp.where(lower, rolled[near, h], plain[far, h]))
                    out_ref[d, c, 0, tile] = jnp.concatenate(keys, axis=0).astype(jnp.bfloat16)
                    out_ref[d, c, 1, tile] = jnp.concatenate(values, axis=0).astype(jnp.bfloat16)
        return carry

    lax.fori_loop(0, part, fill, 0, unroll=2)


def gather_windows(past, block_order, recv):
    blocks = block_order.shape[0]
    part = blocks // 4
    shape = lambda rows, units: (rows, units, 2, past // 4, 16, HEAD)
    return pl.pallas_call(
        functools.partial(gather_kernel, past),
        out_shape=[
            jax.ShapeDtypeStruct(shape(blocks, units), jnp.bfloat16) for _, units in CHUNKS
        ],
        grid_spec=pltpu.PrefetchScalarGridSpec(
            num_scalar_prefetch=1,
            grid=(blocks // part,),
            in_specs=[pl.BlockSpec((blocks, KV_HEADS // 2, 16, HEAD), lambda i, o: (0, 0, 0, 0))],
            out_specs=[
                pl.BlockSpec(shape(part, units), lambda i, o: (i, 0, 0, 0, 0, 0))
                for _, units in CHUNKS
            ],
            scratch_shapes=[
                pltpu.SMEM((blocks,), jnp.int32),
                pltpu.VMEM((blocks, KV_HEADS, 8, HEAD), jnp.float32),
                pltpu.VMEM((blocks, KV_HEADS, 8, HEAD), jnp.float32),
            ],
        ),
        compiler_params=pltpu.CompilerParams(vmem_limit_bytes=VMEM),
        cost_estimate=pl.CostEstimate(flops=0, bytes_accessed=10 << 20, transcendentals=0),
        name="gather_windows",
    )(block_order, recv)


def mark_documents(lengths_ref, place, keys, stacked):
    total_keys, rows = keys.shape[0], stacked.shape[0] // GROUP
    lane = lax.broadcasted_iota(jnp.int32, (8, HEAD), 1)
    row = lax.broadcasted_iota(jnp.int32, (8, HEAD), 0)
    start = jnp.full((8, HEAD), 1 << 30, jnp.int32)
    end = start
    at = 0
    for d in range(lengths_ref.shape[0]):
        start = jnp.where(lane == d, at, start)
        at += lengths_ref[d]
        end = jnp.where(lane == d, at, end)

    def pair(pos_a, pos_b, inside, outside):
        both = [
            jnp.where((pos >= start) & (pos < end), inside, outside) for pos in (pos_a, pos_b)
        ]
        return jnp.concatenate(both, axis=0).astype(jnp.bfloat16)

    past_keys = total_keys - rows
    slots = past_keys // rows
    origins = []
    for slot in range(0, slots, 2):
        block = place - 1 - slot - row // THIN
        origins.append(jnp.where(block >= 0, block * rows + row % THIN, -(1 << 20)))

    def past(i, carry):
        for tile in range(slots // 4):
            to = pl.ds(pl.multiple_of((i * (slots // 4) + tile) * 16, 16), 16)
            pos = [origins[2 * tile + half] + i * THIN for half in range(2)]
            keys[to, HEAD:] = pair(*pos, 0.0, HIDDEN)
        return carry

    lax.fori_loop(0, rows // THIN, past, 0, unroll=4)
    for r in range(0, rows, 16):
        base = place * rows + r + row
        keys[past_keys + r : past_keys + r + 16, HEAD:] = pair(base, base + 8, 0.0, HIDDEN)
        marks = pair(base, base + 8, 1.0, 0.0)
        for g in range(GROUP):
            stacked[g * rows + r : g * rows + r + 16, HEAD:] = marks


def attend_kernel(lengths_ref, order_ref, me_ref, q_ref, k_own, v_own, window, *rest):
    out_ref, keys, values, stacked, scores_a, scores_b, peak_a, peak_b = rest[-8:]
    rows = q_ref.shape[0]
    total_keys = keys.shape[0]
    past_keys = total_keys - rows
    tall = STACK * rows

    @pl.when(pl.program_id(0) == 0)
    def _():
        mark_documents(lengths_ref, order_ref[me_ref[0]], keys, stacked)
        values[:, HEAD:] = jnp.ones((total_keys, HEAD), jnp.bfloat16)

    keys[:past_keys, :HEAD] = window[:, 0, 0].reshape(past_keys, HEAD)
    keys[past_keys:, :HEAD] = k_own[...]
    values[:past_keys, :HEAD] = window[:, 0, 1].reshape(past_keys, HEAD)
    values[past_keys:, :HEAD] = v_own[...]
    for g in range(GROUP):
        stacked[g * rows : (g + 1) * rows, :HEAD] = q_ref[:, g * HEAD : (g + 1) * HEAD]
    scale = math.log2(math.e) / math.sqrt(HEAD)
    tiles = [(t, t + rows) for t in range(0, total_keys, rows)]
    causal = lax.broadcasted_iota(jnp.int32, (tall, rows), 0) % rows >= lax.broadcasted_iota(
        jnp.int32, (tall, rows), 1
    )

    def score(g, scores, peak):
        q = stacked[g * tall : (g + 1) * tall, :]
        most = None
        for a, b in tiles:
            s = lax.dot_general(
                q, keys[a:b, :], (((1,), (1,)), ((), ())), preferred_element_type=jnp.float32
            )
            if a == past_keys:
                s = jnp.where(causal, s, HIDDEN)
            scores[:, a:b] = s
            for lane in range(0, rows, HEAD):
                part = s[:, lane : lane + HEAD]
                most = part if most is None else jnp.maximum(most, part)
        peak[...] = jnp.broadcast_to(jnp.max(most, axis=1, keepdims=True), (tall, HEAD))

    def mix(g, scores, peak):
        most = jnp.concatenate([peak[...]] * (rows // HEAD), axis=1)
        mixed = None
        for a, b in tiles:
            w = jnp.exp2((scores[:, a:b] - most) * scale).astype(jnp.bfloat16)
            part = jnp.dot(w, values[a:b, :], preferred_element_type=jnp.float32)
            mixed = part if mixed is None else mixed + part
        out = (mixed[:, :HEAD] / mixed[:, HEAD:]).astype(jnp.bfloat16)
        for h in range(STACK):
            at = (g * STACK + h) * HEAD
            out_ref[:, at : at + HEAD] = out[h * rows : (h + 1) * rows]

    buffers = ((scores_a, peak_a), (scores_b, peak_b))
    stacks = GROUP // STACK
    score(0, *buffers[0])
    for g in range(stacks):
        if g + 1 < stacks:
            score(g + 1, *buffers[(g + 1) % 2])
        mix(g, *buffers[g % 2])


def attend(first, units, lengths, order, me, queries, own_keys, own_values, window, attended):
    rows, width = queries.shape
    sources, _, _, tiles = window.shape[:4]
    total_keys = sources * tiles * 16 + rows
    tall = STACK * rows
    head = lambda c, *scalars: (0, first + c)
    in_specs = [
        pl.BlockSpec((rows, GROUP * HEAD), head),
        pl.BlockSpec((rows, HEAD), head),
        pl.BlockSpec((rows, HEAD), head),
        pl.BlockSpec((sources, 1, 2, tiles, 16, HEAD), lambda c, *scalars: (0, c, 0, 0, 0, 0)),
    ]
    operands = [lengths, order, me, queries, own_keys, own_values, window]
    aliases = {}
    if attended is not None:
        in_specs.append(pl.BlockSpec(memory_space=pl.ANY))
        aliases = {len(operands): 0}
        operands.append(attended)
    done = units * GROUP * rows * total_keys
    return pl.pallas_call(
        attend_kernel,
        out_shape=jax.ShapeDtypeStruct((rows, width), jnp.bfloat16),
        grid_spec=pltpu.PrefetchScalarGridSpec(
            num_scalar_prefetch=3,
            grid=(units,),
            in_specs=in_specs,
            out_specs=pl.BlockSpec((rows, GROUP * HEAD), head),
            scratch_shapes=[
                pltpu.VMEM((total_keys, 2 * HEAD), jnp.bfloat16),
                pltpu.VMEM((total_keys, 2 * HEAD), jnp.bfloat16),
                pltpu.VMEM((GROUP * rows, 2 * HEAD), jnp.bfloat16),
                pltpu.VMEM((tall, total_keys), jnp.float32),
                pltpu.VMEM((tall, total_keys), jnp.float32),
                pltpu.VMEM((tall, HEAD), jnp.float32),
                pltpu.VMEM((tall, HEAD), jnp.float32),
            ],
        ),
        input_output_aliases=aliases,
        compiler_params=pltpu.CompilerParams(vmem_limit_bytes=VMEM),
        cost_estimate=pl.CostEstimate(
            flops=done * 2 * 4 * HEAD, bytes_accessed=units << 21, transcendentals=done
        ),
        name="attend",
    )(*operands)


def body(queries, rotated_key_rows, stored_value_rows, doc_lengths, block_order):
    axes = ("context", "tensor")
    past = 8
    me = lax.axis_index("context") * lax.axis_size("tensor") + lax.axis_index("tensor")
    me = me.astype(jnp.int32).reshape(1)
    pieces = cut_pieces(rotated_key_rows, stored_value_rows)
    pieces, me = lax.optimization_barrier((pieces, me))
    recv = lax.all_to_all(pieces, axes, split_axis=0, concat_axis=0, tiled=True)
    sends = gather_windows(past, block_order, recv)
    sends, me = lax.optimization_barrier((sends, me))
    window = lax.all_to_all(sends[0], axes, split_axis=0, concat_axis=0, tiled=True)
    window, me, sends = lax.optimization_barrier((window, me, sends))
    own = (queries, rotated_key_rows, stored_value_rows)
    attended = None
    for step, (first, units) in enumerate(CHUNKS):
        here = window
        if step + 1 < len(CHUNKS):
            send = sends[step + 1]
            if step:
                send, attended = lax.optimization_barrier((send, attended))
            window = lax.all_to_all(send, axes, split_axis=0, concat_axis=0, tiled=True)
        attended = attend(first, units, doc_lengths, block_order, me, *own, here, attended)
    return attended


def solution(mesh):
    rows = P(("dp", "context", "tensor"), None)
    return jax.shard_map(
        body,
        mesh=mesh,
        in_specs=(rows, rows, rows, P("dp"), P("dp")),
        out_specs=rows,
        check_vma=False,
    )
```

```python
import functools
import math

import jax
import jax.numpy as jnp
from jax import lax
from jax.experimental import pallas as pl
from jax.experimental.pallas import tpu as pltpu
from jax.sharding import PartitionSpec as P

HEAD = 128
GROUP = 8
KV_HEADS = 8
HIDDEN = -1e30
FIRST = 11
THIN = 4
STACK = 4
VMEM = 62 << 20


def pieces_kernel(k_ref, v_ref, out_ref):
    tall = 16
    lower = lax.broadcasted_iota(jnp.int32, (8, HEAD), 0) < THIN

    def some_rows(r, carry):
        rows = pl.ds(pl.multiple_of(r * tall, tall), tall)
        for pair in range(KV_HEADS // 2):
            halves = []
            for h in (2 * pair, 2 * pair + 1):
                k = k_ref[rows, h * HEAD : (h + 1) * HEAD].astype(jnp.float32)
                v = v_ref[rows, h * HEAD : (h + 1) * HEAD].astype(jnp.float32)
                parts = []
                for at in (0, 8):
                    k8, v8 = k[at : at + 8], v[at : at + 8]
                    parts.append(jnp.where(lower, k8, pltpu.roll(v8, THIN, 0)))
                    parts.append(jnp.where(lower, pltpu.roll(k8, THIN, 0), v8))
                halves.append(parts)
            for j in range(tall // THIN):
                both = jnp.concatenate([halves[0][j], halves[1][j]], axis=0)
                out_ref[r * (tall // THIN) + j, pair] = both.astype(jnp.bfloat16)
        return carry

    lax.fori_loop(0, k_ref.shape[0] // tall, some_rows, 0, unroll=2)


def cut_pieces(own_keys, own_values):
    rows, width = own_keys.shape
    blocks = rows // THIN
    steps = 4
    return pl.pallas_call(
        pieces_kernel,
        out_shape=jax.ShapeDtypeStruct((blocks, KV_HEADS // 2, 16, HEAD), jnp.bfloat16),
        grid=(steps,),
        in_specs=[pl.BlockSpec((rows // steps, width), lambda i: (i, 0))] * 2,
        out_specs=pl.BlockSpec(
            (blocks // steps, KV_HEADS // 2, 16, HEAD), lambda i: (i, 0, 0, 0)
        ),
        compiler_params=pltpu.CompilerParams(vmem_limit_bytes=VMEM),
        cost_estimate=pl.CostEstimate(flops=0, bytes_accessed=2 << 20, transcendentals=0),
        name="cut_pieces",
    )(own_keys, own_values)


def gather_kernel(past, order_ref, recv_ref, *rest):
    out_refs, (inverse, plain, rolled) = rest[:-3], rest[-3:]
    blocks = order_ref.shape[0]
    part = out_refs[0].shape[0]
    step = pl.program_id(0)
    lower = lax.broadcasted_iota(jnp.int32, (8, HEAD), 0) < THIN

    @pl.when(step == 0)
    def _():
        for j in range(blocks):
            inverse[order_ref[j]] = j

        def open_block(j, carry):
            for pair in range(KV_HEADS // 2):
                x = recv_ref[j, pair].astype(jnp.float32)
                for half in range(2):
                    h = 2 * pair + half
                    x8 = x[8 * half : 8 * half + 8]
                    plain[j, h] = x8
                    rolled[j, h] = pltpu.roll(x8, THIN, 0)
            return carry

        lax.fori_loop(0, blocks, open_block, 0, unroll=4)

    def fill(d, carry):
        s = order_ref[step * part + d]
        held = [inverse[jnp.maximum(s - 1 - slot, 0)] for slot in range(past)]
        for h in range(KV_HEADS):
            for tile in range(past // 4):
                keys, values = [], []
                for slot in (4 * tile, 4 * tile + 2):
                    near, far = held[slot], held[slot + 1]
                    keys.append(jnp.where(lower, plain[near, h], rolled[far, h]))
                    values.append(jnp.where(lower, rolled[near, h], plain[far, h]))
                for f, rows in ((2 * h, keys), (2 * h + 1, values)):
                    out_ref, at = (out_refs[0], f) if f < FIRST else (out_refs[1], f - FIRST)
                    out_ref[d, at, tile] = jnp.concatenate(rows, axis=0).astype(jnp.bfloat16)
        return carry

    lax.fori_loop(0, part, fill, 0, unroll=2)


def gather_windows(past, block_order, recv):
    blocks = block_order.shape[0]
    part = blocks // 4
    sizes = (FIRST, 2 * KV_HEADS - FIRST)
    shape = lambda rows, size: (rows, size, past // 4, 16, HEAD)
    return pl.pallas_call(
        functools.partial(gather_kernel, past),
        out_shape=[jax.ShapeDtypeStruct(shape(blocks, size), jnp.bfloat16) for size in sizes],
        grid_spec=pltpu.PrefetchScalarGridSpec(
            num_scalar_prefetch=1,
            grid=(blocks // part,),
            in_specs=[pl.BlockSpec((blocks, KV_HEADS // 2, 16, HEAD), lambda i, o: (0, 0, 0, 0))],
            out_specs=[
                pl.BlockSpec(shape(part, size), lambda i, o: (i, 0, 0, 0, 0)) for size in sizes
            ],
            scratch_shapes=[
                pltpu.SMEM((blocks,), jnp.int32),
                pltpu.VMEM((blocks, KV_HEADS, 8, HEAD), jnp.float32),
                pltpu.VMEM((blocks, KV_HEADS, 8, HEAD), jnp.float32),
            ],
        ),
        compiler_params=pltpu.CompilerParams(vmem_limit_bytes=24 << 20),
        cost_estimate=pl.CostEstimate(flops=0, bytes_accessed=10 << 20, transcendentals=0),
        name="gather_windows",
    )(block_order, recv)


def mark_documents(lengths_ref, place, keys, stacked):
    total_keys, rows = keys.shape[0], stacked.shape[0] // GROUP
    lane = lax.broadcasted_iota(jnp.int32, (8, HEAD), 1)
    row = lax.broadcasted_iota(jnp.int32, (8, HEAD), 0)
    start = jnp.full((8, HEAD), 1 << 30, jnp.int32)
    end = start
    at = 0
    for d in range(lengths_ref.shape[0]):
        start = jnp.where(lane == d, at, start)
        at += lengths_ref[d]
        end = jnp.where(lane == d, at, end)

    def pair(pos_a, pos_b, inside, outside):
        both = [
            jnp.where((pos >= start) & (pos < end), inside, outside) for pos in (pos_a, pos_b)
        ]
        return jnp.concatenate(both, axis=0).astype(jnp.bfloat16)

    past_keys = total_keys - rows
    slots = past_keys // rows
    origins = []
    for slot in range(0, slots, 2):
        block = place - 1 - slot - row // THIN
        origins.append(jnp.where(block >= 0, block * rows + row % THIN, -(1 << 20)))

    def past(i, carry):
        for tile in range(slots // 4):
            to = pl.ds(pl.multiple_of((i * (slots // 4) + tile) * 16, 16), 16)
            pos = [origins[2 * tile + half] + i * THIN for half in range(2)]
            keys[to, HEAD:] = pair(*pos, 0.0, HIDDEN)
        return carry

    lax.fori_loop(0, rows // THIN, past, 0, unroll=16)
    for r in range(0, rows, 16):
        base = place * rows + r + row
        keys[past_keys + r : past_keys + r + 16, HEAD:] = pair(base, base + 8, 0.0, HIDDEN)
        marks = pair(base, base + 8, 1.0, 0.0)
        for g in range(GROUP):
            stacked[g * rows + r : g * rows + r + 16, HEAD:] = marks


def attend_kernel(early, lengths_ref, order_ref, me_ref, q_ref, k_own, v_own, *rest):
    out_ref, keys, values, stacked, scores_a, scores_b, peak_a, peak_b = rest[-8:]
    k_window, v_window = rest[:2]
    rows = q_ref.shape[0]
    total_keys = keys.shape[0]
    past_keys = total_keys - rows
    tall = STACK * rows

    @pl.when(pl.program_id(0) == 0)
    def _():
        mark_documents(lengths_ref, order_ref[me_ref[0]], keys, stacked)
        values[:, HEAD:] = jnp.ones((total_keys, HEAD), jnp.bfloat16)

    if early:
        keys[:past_keys, :HEAD] = k_window[...].reshape(past_keys, HEAD)
    else:
        k_early = rest[2]

        @pl.when(pl.program_id(0) == 0)
        def _():
            keys[:past_keys, :HEAD] = k_early[...].reshape(past_keys, HEAD)

        @pl.when(pl.program_id(0) > 0)
        def _():
            keys[:past_keys, :HEAD] = k_window[...].reshape(past_keys, HEAD)

    keys[past_keys:, :HEAD] = k_own[...]
    values[:past_keys, :HEAD] = v_window[...].reshape(past_keys, HEAD)
    values[past_keys:, :HEAD] = v_own[...]
    for g in range(GROUP):
        stacked[g * rows : (g + 1) * rows, :HEAD] = q_ref[:, g * HEAD : (g + 1) * HEAD]
    scale = math.log2(math.e) / math.sqrt(HEAD)
    tiles = [(t, t + rows) for t in range(0, total_keys, rows)]
    causal = lax.broadcasted_iota(jnp.int32, (tall, rows), 0) % rows >= lax.broadcasted_iota(
        jnp.int32, (tall, rows), 1
    )

    def score(g, scores, peak):
        q = stacked[g * tall : (g + 1) * tall, :]
        most = None
        for a, b in tiles:
            s = lax.dot_general(
                q, keys[a:b, :], (((1,), (1,)), ((), ())), preferred_element_type=jnp.float32
            )
            if a == past_keys:
                s = jnp.where(causal, s, HIDDEN)
            scores[:, a:b] = s
            for lane in range(0, rows, HEAD):
                part = s[:, lane : lane + HEAD]
                most = part if most is None else jnp.maximum(most, part)
        peak[...] = jnp.broadcast_to(jnp.max(most, axis=1, keepdims=True), (tall, HEAD))

    def mix(g, scores, peak):
        most = jnp.concatenate([peak[...]] * (rows // HEAD), axis=1)
        mixed = None
        for a, b in tiles:
            w = jnp.exp2((scores[:, a:b] - most) * scale).astype(jnp.bfloat16)
            part = jnp.dot(w, values[a:b, :], preferred_element_type=jnp.float32)
            mixed = part if mixed is None else mixed + part
        out = (mixed[:, :HEAD] / mixed[:, HEAD:]).astype(jnp.bfloat16)
        for h in range(STACK):
            at = (g * STACK + h) * HEAD
            out_ref[:, at : at + HEAD] = out[h * rows : (h + 1) * rows]

    buffers = ((scores_a, peak_a), (scores_b, peak_b))
    stacks = GROUP // STACK
    score(0, *buffers[0])
    for g in range(stacks):
        if g + 1 < stacks:
            score(g + 1, *buffers[(g + 1) % 2])
        mix(g, *buffers[g % 2])


def attend(lengths, order, me, queries, own_keys, own_values, windows, attended):
    rows, width = queries.shape
    early = attended is None
    first = 0 if early else FIRST // 2
    units = FIRST // 2 if early else KV_HEADS - first
    sources, _, tiles = windows[0].shape[:3]
    total_keys = sources * tiles * 16 + rows
    tall = STACK * rows
    head = lambda c, *scalars: (0, first + c)
    half = lambda index: pl.BlockSpec(
        (sources, 1, tiles, 16, HEAD), lambda c, *scalars: (0, index(c), 0, 0, 0)
    )
    in_specs = [
        pl.BlockSpec((rows, GROUP * HEAD), head),
        pl.BlockSpec((rows, HEAD), head),
        pl.BlockSpec((rows, HEAD), head),
    ]
    operands = [lengths, order, me, queries, own_keys, own_values]
    aliases = {}
    if early:
        in_specs += [half(lambda c: 2 * c), half(lambda c: 2 * c + 1)]
        operands += [windows[0]] * 2
    else:
        in_specs += [half(lambda c: jnp.maximum(2 * c - 1, 1)), half(lambda c: 2 * c)]
        in_specs += [half(lambda c: FIRST - 1), pl.BlockSpec(memory_space=pl.ANY)]
        operands += [windows[1], windows[1], windows[0], attended]
        aliases = {len(operands) - 1: 0}
    done = units * GROUP * rows * total_keys
    return pl.pallas_call(
        functools.partial(attend_kernel, early),
        out_shape=jax.ShapeDtypeStruct((rows, width), jnp.bfloat16),
        grid_spec=pltpu.PrefetchScalarGridSpec(
            num_scalar_prefetch=3,
            grid=(units,),
            in_specs=in_specs,
            out_specs=pl.BlockSpec((rows, GROUP * HEAD), head),
            scratch_shapes=[
                pltpu.VMEM((total_keys, 2 * HEAD), jnp.bfloat16),
                pltpu.VMEM((total_keys, 2 * HEAD), jnp.bfloat16),
                pltpu.VMEM((GROUP * rows, 2 * HEAD), jnp.bfloat16),
                pltpu.VMEM((tall, total_keys), jnp.float32),
                pltpu.VMEM((tall, total_keys), jnp.float32),
                pltpu.VMEM((tall, HEAD), jnp.float32),
                pltpu.VMEM((tall, HEAD), jnp.float32),
            ],
        ),
        input_output_aliases=aliases,
        compiler_params=pltpu.CompilerParams(vmem_limit_bytes=VMEM),
        cost_estimate=pl.CostEstimate(
            flops=done * 2 * 4 * HEAD, bytes_accessed=units << 21, transcendentals=done
        ),
        name="attend",
    )(*operands)


def body(queries, rotated_key_rows, stored_value_rows, doc_lengths, block_order):
    axes = ("context", "tensor")
    past = 8
    me = lax.axis_index("context") * lax.axis_size("tensor") + lax.axis_index("tensor")
    me = me.astype(jnp.int32).reshape(1)
    pieces = cut_pieces(rotated_key_rows, stored_value_rows)
    pieces, me = lax.optimization_barrier((pieces, me))
    recv = lax.all_to_all(pieces, axes, split_axis=0, concat_axis=0, tiled=True)
    sends = gather_windows(past, block_order, recv)
    sends, me = lax.optimization_barrier((sends, me))
    window = lax.all_to_all(sends[0], axes, split_axis=0, concat_axis=0, tiled=True)
    window, me, send = lax.optimization_barrier((window, me, sends[1]))
    late = lax.all_to_all(send, axes, split_axis=0, concat_axis=0, tiled=True)
    own = (queries, rotated_key_rows, stored_value_rows)
    attended = attend(doc_lengths, block_order, me, *own, (window,), None)
    return attend(doc_lengths, block_order, me, *own, (window, late), attended)


def solution(mesh):
    rows = P(("dp", "context", "tensor"), None)
    return jax.shard_map(
        body,
        mesh=mesh,
        in_specs=(rows, rows, rows, P("dp"), P("dp")),
        out_specs=rows,
        check_vma=False,
    )
```

```python
import functools
import math

import jax
import jax.numpy as jnp
from jax import lax
from jax.experimental import pallas as pl
from jax.experimental.pallas import tpu as pltpu
from jax.sharding import PartitionSpec as P

HEAD = 128
GROUP = 8
KV_HEADS = 8
HIDDEN = -1e30
FIRST = 11
THIN = 4
STACK = 4
VMEM = 62 << 20


def pieces_kernel(k_hbm, v_hbm, out_hbm, k_ref, v_ref, out_ref, sems):
    tall = 16
    parts = sems.shape[1]
    part = k_ref.shape[0] // parts
    lower = lax.broadcasted_iota(jnp.int32, (8, HEAD), 0) < THIN
    copies = []
    for p in range(parts):
        rows = pl.ds(p * part, part)
        copies.append(
            [
                pltpu.make_async_copy(hbm.at[rows], held.at[rows], sems.at[i, p])
                for i, (hbm, held) in enumerate(((k_hbm, k_ref), (v_hbm, v_ref)))
            ]
        )
        for copy in copies[-1]:
            copy.start()

    def some_rows(r, carry):
        rows = pl.ds(pl.multiple_of(r * tall, tall), tall)
        for pair in range(KV_HEADS // 2):
            halves = []
            for h in (2 * pair, 2 * pair + 1):
                k = k_ref[rows, h * HEAD : (h + 1) * HEAD].astype(jnp.float32)
                v = v_ref[rows, h * HEAD : (h + 1) * HEAD].astype(jnp.float32)
                pieces = []
                for at in (0, 8):
                    k8, v8 = k[at : at + 8], v[at : at + 8]
                    pieces.append(jnp.where(lower, k8, pltpu.roll(v8, THIN, 0)))
                    pieces.append(jnp.where(lower, pltpu.roll(k8, THIN, 0), v8))
                halves.append(pieces)
            for j in range(tall // THIN):
                both = jnp.concatenate([halves[0][j], halves[1][j]], axis=0)
                out_ref[r * (tall // THIN) + j, pair] = both.astype(jnp.bfloat16)
        return carry

    for p in range(parts):
        for copy in copies[p]:
            copy.wait()
        lax.fori_loop(p * part // tall, (p + 1) * part // tall, some_rows, 0, unroll=True)
        to = pl.ds(p * part // THIN, part // THIN)
        copies[p].append(pltpu.make_async_copy(out_ref.at[to], out_hbm.at[to], sems.at[2, p]))
        copies[p][-1].start()
    for p in range(parts):
        copies[p][-1].wait()


def cut_pieces(own_keys, own_values):
    rows, width = own_keys.shape
    blocks = rows // THIN
    return pl.pallas_call(
        pieces_kernel,
        out_shape=jax.ShapeDtypeStruct((blocks, KV_HEADS // 2, 16, HEAD), jnp.bfloat16),
        in_specs=[pl.BlockSpec(memory_space=pltpu.HBM)] * 2,
        out_specs=pl.BlockSpec(memory_space=pltpu.HBM),
        scratch_shapes=[
            pltpu.VMEM((rows, width), jnp.bfloat16),
            pltpu.VMEM((rows, width), jnp.bfloat16),
            pltpu.VMEM((blocks, KV_HEADS // 2, 16, HEAD), jnp.bfloat16),
            pltpu.SemaphoreType.DMA((3, 4)),
        ],
        compiler_params=pltpu.CompilerParams(vmem_limit_bytes=VMEM),
        cost_estimate=pl.CostEstimate(flops=0, bytes_accessed=2 << 20, transcendentals=0),
        name="cut_pieces",
    )(own_keys, own_values)


def gather_kernel(past, order_ref, recv_ref, early_ref, late_hbm, inverse, plain, rolled, late, sems):
    blocks = order_ref.shape[0]
    parts = sems.shape[0]
    part = blocks // parts
    lower = lax.broadcasted_iota(jnp.int32, (8, HEAD), 0) < THIN
    for j in range(blocks):
        inverse[order_ref[j]] = j

    def open_block(j, carry):
        for pair in range(KV_HEADS // 2):
            x = recv_ref[j, pair].astype(jnp.float32)
            for half in range(2):
                h = 2 * pair + half
                x8 = x[8 * half : 8 * half + 8]
                plain[j, h] = x8
                rolled[j, h] = pltpu.roll(x8, THIN, 0)
        return carry

    lax.fori_loop(0, blocks, open_block, 0, unroll=4)

    def fill(d, carry):
        s = order_ref[d]
        held = [inverse[jnp.maximum(s - 1 - slot, 0)] for slot in range(past)]
        for h in range(KV_HEADS):
            for tile in range(past // 4):
                keys, values = [], []
                for slot in (4 * tile, 4 * tile + 2):
                    near, far = held[slot], held[slot + 1]
                    keys.append(jnp.where(lower, plain[near, h], rolled[far, h]))
                    values.append(jnp.where(lower, rolled[near, h], plain[far, h]))
                for f, rows in ((2 * h, keys), (2 * h + 1, values)):
                    to, at = (early_ref, f) if f < FIRST else (late, f - FIRST)
                    to[d, at, tile] = jnp.concatenate(rows, axis=0).astype(jnp.bfloat16)
        return carry

    copies = []
    for p in range(parts):
        lax.fori_loop(p * part, (p + 1) * part, fill, 0, unroll=2)
        rows = pl.ds(p * part, part)
        copies.append(pltpu.make_async_copy(late.at[rows], late_hbm.at[rows], sems.at[p]))
        copies[-1].start()
    for copy in copies:
        copy.wait()


def gather_windows(past, block_order, recv):
    blocks = block_order.shape[0]
    shape = lambda size: (blocks, size, past // 4, 16, HEAD)
    early, late = shape(FIRST), shape(2 * KV_HEADS - FIRST)
    return pl.pallas_call(
        functools.partial(gather_kernel, past),
        out_shape=[
            jax.ShapeDtypeStruct(early, jnp.bfloat16),
            jax.ShapeDtypeStruct(late, jnp.bfloat16),
        ],
        in_specs=[
            pl.BlockSpec(memory_space=pltpu.SMEM),
            pl.BlockSpec(memory_space=pltpu.VMEM),
        ],
        out_specs=[
            pl.BlockSpec(memory_space=pltpu.VMEM),
            pl.BlockSpec(memory_space=pltpu.HBM),
        ],
        scratch_shapes=[
            pltpu.SMEM((blocks,), jnp.int32),
            pltpu.VMEM((blocks, KV_HEADS, 8, HEAD), jnp.float32),
            pltpu.VMEM((blocks, KV_HEADS, 8, HEAD), jnp.float32),
            pltpu.VMEM(late, jnp.bfloat16),
            pltpu.SemaphoreType.DMA((4,)),
        ],
        compiler_params=pltpu.CompilerParams(vmem_limit_bytes=24 << 20),
        cost_estimate=pl.CostEstimate(flops=0, bytes_accessed=10 << 20, transcendentals=0),
        name="gather_windows",
    )(block_order, recv)


def mark_documents(lengths_ref, place, keys, stacked):
    total_keys, rows = keys.shape[0], stacked.shape[0] // GROUP
    lane = lax.broadcasted_iota(jnp.int32, (8, HEAD), 1)
    row = lax.broadcasted_iota(jnp.int32, (8, HEAD), 0)
    start = jnp.full((8, HEAD), 1 << 30, jnp.int32)
    end = start
    at = 0
    for d in range(lengths_ref.shape[0]):
        start = jnp.where(lane == d, at, start)
        at += lengths_ref[d]
        end = jnp.where(lane == d, at, end)

    def pair(pos_a, pos_b, inside, outside):
        both = [
            jnp.where((pos >= start) & (pos < end), inside, outside) for pos in (pos_a, pos_b)
        ]
        return jnp.concatenate(both, axis=0).astype(jnp.bfloat16)

    past_keys = total_keys - rows
    slots = past_keys // rows
    origins = []
    for slot in range(0, slots, 2):
        block = place - 1 - slot - row // THIN
        origins.append(jnp.where(block >= 0, block * rows + row % THIN, -(1 << 20)))

    def past(i, carry):
        for tile in range(slots // 4):
            to = pl.ds(pl.multiple_of((i * (slots // 4) + tile) * 16, 16), 16)
            pos = [origins[2 * tile + half] + i * THIN for half in range(2)]
            keys[to, HEAD:] = pair(*pos, 0.0, HIDDEN)
        return carry

    lax.fori_loop(0, rows // THIN, past, 0, unroll=16)
    for r in range(0, rows, 16):
        base = place * rows + r + row
        keys[past_keys + r : past_keys + r + 16, HEAD:] = pair(base, base + 8, 0.0, HIDDEN)
        marks = pair(base, base + 8, 1.0, 0.0)
        for g in range(GROUP):
            stacked[g * rows + r : g * rows + r + 16, HEAD:] = marks


def attend_kernel(early, lengths_ref, order_ref, me_ref, q_ref, k_own, v_own, *rest):
    out_ref, keys, values, stacked, scores_a, scores_b, peak_a, peak_b = rest[-8:]
    k_window, v_window = rest[0:2], rest[2:4]
    rows = q_ref.shape[0]
    total_keys = keys.shape[0]
    past_keys = total_keys - rows
    tall = STACK * rows

    @pl.when(pl.program_id(0) == 0)
    def _():
        mark_documents(lengths_ref, order_ref[me_ref[0]], keys, stacked)
        values[:, HEAD:] = jnp.ones((total_keys, HEAD), jnp.bfloat16)

    part = past_keys // 2

    def place_keys(halves):
        for p, ref in enumerate(halves):
            keys[p * part : (p + 1) * part, :HEAD] = ref[...].reshape(part, HEAD)

    if early:
        place_keys(k_window)
    else:
        pl.when(pl.program_id(0) == 0)(lambda: place_keys(rest[4:6]))
        pl.when(pl.program_id(0) > 0)(lambda: place_keys(k_window))
    keys[past_keys:, :HEAD] = k_own[...]
    for p, ref in enumerate(v_window):
        values[p * part : (p + 1) * part, :HEAD] = ref[...].reshape(part, HEAD)
    values[past_keys:, :HEAD] = v_own[...]
    for g in range(GROUP):
        stacked[g * rows : (g + 1) * rows, :HEAD] = q_ref[:, g * HEAD : (g + 1) * HEAD]
    scale = math.log2(math.e) / math.sqrt(HEAD)
    tiles = [(t, t + rows) for t in range(0, total_keys, rows)]
    causal = lax.broadcasted_iota(jnp.int32, (tall, rows), 0) % rows >= lax.broadcasted_iota(
        jnp.int32, (tall, rows), 1
    )

    def score(g, scores, peak):
        q = stacked[g * tall : (g + 1) * tall, :]
        most = None
        for a, b in tiles:
            s = lax.dot_general(
                q, keys[a:b, :], (((1,), (1,)), ((), ())), preferred_element_type=jnp.float32
            )
            if a == past_keys:
                s = jnp.where(causal, s, HIDDEN)
            scores[:, a:b] = s
            for lane in range(0, rows, HEAD):
                part = s[:, lane : lane + HEAD]
                most = part if most is None else jnp.maximum(most, part)
        peak[...] = jnp.broadcast_to(jnp.max(most, axis=1, keepdims=True), (tall, HEAD))

    def mix(g, scores, peak):
        most = jnp.concatenate([peak[...]] * (rows // HEAD), axis=1)
        mixed = None
        for a, b in tiles:
            w = jnp.exp2((scores[:, a:b] - most) * scale).astype(jnp.bfloat16)
            part = jnp.dot(w, values[a:b, :], preferred_element_type=jnp.float32)
            mixed = part if mixed is None else mixed + part
        out = (mixed[:, :HEAD] / mixed[:, HEAD:]).astype(jnp.bfloat16)
        for h in range(STACK):
            at = (g * STACK + h) * HEAD
            out_ref[:, at : at + HEAD] = out[h * rows : (h + 1) * rows]

    buffers = ((scores_a, peak_a), (scores_b, peak_b))
    stacks = GROUP // STACK
    score(0, *buffers[0])
    for g in range(stacks):
        if g + 1 < stacks:
            score(g + 1, *buffers[(g + 1) % 2])
        mix(g, *buffers[g % 2])


def attend(lengths, order, me, queries, own_keys, own_values, windows, attended):
    rows, width = queries.shape
    early = attended is None
    first = 0 if early else FIRST // 2
    units = FIRST // 2 if early else KV_HEADS - first
    sources, _, tiles = windows[0].shape[:3]
    total_keys = sources * tiles * 16 + rows
    tall = STACK * rows
    head = lambda c, *scalars: (0, first + c)
    half = lambda index: [
        pl.BlockSpec(
            (sources // 2, 1, tiles, 16, HEAD),
            lambda c, *scalars, p=p: (p, index(c), 0, 0, 0),
        )
        for p in range(2)
    ]
    in_specs = [
        pl.BlockSpec((rows, GROUP * HEAD), head),
        pl.BlockSpec((rows, HEAD), head),
        pl.BlockSpec((rows, HEAD), head),
    ]
    operands = [lengths, order, me, queries, own_keys, own_values]
    aliases = {}
    if early:
        in_specs += half(lambda c: 2 * c) + half(lambda c: 2 * c + 1)
        operands += [windows[0]] * 4
    else:
        in_specs += half(lambda c: jnp.maximum(2 * c - 1, 1)) + half(lambda c: 2 * c)
        in_specs += half(lambda c: FIRST - 1) + [pl.BlockSpec(memory_space=pl.ANY)]
        operands += [windows[1]] * 4 + [windows[0]] * 2 + [attended]
        aliases = {len(operands) - 1: 0}
    done = units * GROUP * rows * total_keys
    return pl.pallas_call(
        functools.partial(attend_kernel, early),
        out_shape=jax.ShapeDtypeStruct((rows, width), jnp.bfloat16),
        grid_spec=pltpu.PrefetchScalarGridSpec(
            num_scalar_prefetch=3,
            grid=(units,),
            in_specs=in_specs,
            out_specs=pl.BlockSpec((rows, GROUP * HEAD), head),
            scratch_shapes=[
                pltpu.VMEM((total_keys, 2 * HEAD), jnp.bfloat16),
                pltpu.VMEM((total_keys, 2 * HEAD), jnp.bfloat16),
                pltpu.VMEM((GROUP * rows, 2 * HEAD), jnp.bfloat16),
                pltpu.VMEM((tall, total_keys), jnp.float32),
                pltpu.VMEM((tall, total_keys), jnp.float32),
                pltpu.VMEM((tall, HEAD), jnp.float32),
                pltpu.VMEM((tall, HEAD), jnp.float32),
            ],
        ),
        input_output_aliases=aliases,
        compiler_params=pltpu.CompilerParams(vmem_limit_bytes=VMEM),
        cost_estimate=pl.CostEstimate(
            flops=done * 2 * 4 * HEAD, bytes_accessed=units << 21, transcendentals=done
        ),
        name="attend",
    )(*operands)


def body(queries, rotated_key_rows, stored_value_rows, doc_lengths, block_order):
    axes = ("context", "tensor")
    past = 8
    me = lax.axis_index("context") * lax.axis_size("tensor") + lax.axis_index("tensor")
    me = me.astype(jnp.int32).reshape(1)
    pieces = cut_pieces(rotated_key_rows, stored_value_rows)
    pieces, me = lax.optimization_barrier((pieces, me))
    recv = lax.all_to_all(pieces, axes, split_axis=0, concat_axis=0, tiled=True)
    sends = gather_windows(past, block_order, recv)
    sends, me = lax.optimization_barrier((sends, me))
    window = lax.all_to_all(sends[0], axes, split_axis=0, concat_axis=0, tiled=True)
    window, me, send = lax.optimization_barrier((window, me, sends[1]))
    late = lax.all_to_all(send, axes, split_axis=0, concat_axis=0, tiled=True)
    own = (queries, rotated_key_rows, stored_value_rows)
    attended = attend(doc_lengths, block_order, me, *own, (window,), None)
    return attend(doc_lengths, block_order, me, *own, (window, late), attended)


def solution(mesh):
    rows = P(("dp", "context", "tensor"), None)
    return jax.shard_map(
        body,
        mesh=mesh,
        in_specs=(rows, rows, rows, P("dp"), P("dp")),
        out_specs=rows,
        check_vma=False,
    )
```

```python
import functools
import math

import jax
import jax.numpy as jnp
from jax import lax
from jax.experimental import pallas as pl
from jax.experimental.pallas import tpu as pltpu
from jax.sharding import PartitionSpec as P

HEAD = 128
GROUP = 8
KV_HEADS = 8
HIDDEN = -1e30
FIRST = 11
THIN = 4
STACK = 4
VMEM = 62 << 20


def pieces_kernel(k_hbm, v_hbm, out_hbm, k_ref, v_ref, out_ref, sems):
    tall = 16
    parts = sems.shape[1]
    part = k_ref.shape[0] // parts
    lower = lax.broadcasted_iota(jnp.int32, (8, HEAD), 0) < THIN
    copies = []
    for p in range(parts):
        rows = pl.ds(p * part, part)
        copies.append(
            [
                pltpu.make_async_copy(hbm.at[rows], held.at[rows], sems.at[i, p])
                for i, (hbm, held) in enumerate(((k_hbm, k_ref), (v_hbm, v_ref)))
            ]
        )
        for copy in copies[-1]:
            copy.start()

    def some_rows(r, carry):
        rows = pl.ds(pl.multiple_of(r * tall, tall), tall)
        for pair in range(KV_HEADS // 2):
            halves = []
            for h in (2 * pair, 2 * pair + 1):
                k = k_ref[rows, h * HEAD : (h + 1) * HEAD].astype(jnp.float32)
                v = v_ref[rows, h * HEAD : (h + 1) * HEAD].astype(jnp.float32)
                pieces = []
                for at in (0, 8):
                    k8, v8 = k[at : at + 8], v[at : at + 8]
                    pieces.append(jnp.where(lower, k8, pltpu.roll(v8, THIN, 0)))
                    pieces.append(jnp.where(lower, pltpu.roll(k8, THIN, 0), v8))
                halves.append(pieces)
            for j in range(tall // THIN):
                both = jnp.concatenate([halves[0][j], halves[1][j]], axis=0)
                out_ref[r * (tall // THIN) + j, pair] = both.astype(jnp.bfloat16)
        return carry

    for p in range(parts):
        for copy in copies[p]:
            copy.wait()
        lax.fori_loop(p * part // tall, (p + 1) * part // tall, some_rows, 0, unroll=True)
        to = pl.ds(p * part // THIN, part // THIN)
        copies[p].append(pltpu.make_async_copy(out_ref.at[to], out_hbm.at[to], sems.at[2, p]))
        copies[p][-1].start()
    for p in range(parts):
        copies[p][-1].wait()


def cut_pieces(own_keys, own_values):
    rows, width = own_keys.shape
    blocks = rows // THIN
    return pl.pallas_call(
        pieces_kernel,
        out_shape=jax.ShapeDtypeStruct((blocks, KV_HEADS // 2, 16, HEAD), jnp.bfloat16),
        in_specs=[pl.BlockSpec(memory_space=pltpu.HBM)] * 2,
        out_specs=pl.BlockSpec(memory_space=pltpu.HBM),
        scratch_shapes=[
            pltpu.VMEM((rows, width), jnp.bfloat16),
            pltpu.VMEM((rows, width), jnp.bfloat16),
            pltpu.VMEM((blocks, KV_HEADS // 2, 16, HEAD), jnp.bfloat16),
            pltpu.SemaphoreType.DMA((3, 4)),
        ],
        compiler_params=pltpu.CompilerParams(vmem_limit_bytes=VMEM),
        cost_estimate=pl.CostEstimate(flops=0, bytes_accessed=2 << 20, transcendentals=0),
        name="cut_pieces",
    )(own_keys, own_values)


def gather_kernel(past, order_ref, recv_ref, early_ref, late_hbm, inverse, plain, rolled, late, sems):
    blocks = order_ref.shape[0]
    parts = sems.shape[0]
    part = blocks // parts
    lower = lax.broadcasted_iota(jnp.int32, (8, HEAD), 0) < THIN
    for j in range(blocks):
        inverse[order_ref[j]] = j

    def open_block(j, carry):
        for pair in range(KV_HEADS // 2):
            x = recv_ref[j, pair].astype(jnp.float32)
            for half in range(2):
                h = 2 * pair + half
                x8 = x[8 * half : 8 * half + 8]
                plain[j, h] = x8
                rolled[j, h] = pltpu.roll(x8, THIN, 0)
        return carry

    lax.fori_loop(0, blocks, open_block, 0, unroll=4)

    def fill(d, carry):
        s = order_ref[d]
        held = [inverse[jnp.maximum(s - 1 - slot, 0)] for slot in range(past)]
        for h in range(KV_HEADS):
            for tile in range(past // 4):
                keys, values = [], []
                for slot in (4 * tile, 4 * tile + 2):
                    near, far = held[slot], held[slot + 1]
                    keys.append(jnp.where(lower, plain[near, h], rolled[far, h]))
                    values.append(jnp.where(lower, rolled[near, h], plain[far, h]))
                for f, rows in ((2 * h, keys), (2 * h + 1, values)):
                    to, at = (early_ref, f) if f < FIRST else (late, f - FIRST)
                    to[d, at, tile] = jnp.concatenate(rows, axis=0).astype(jnp.bfloat16)
        return carry

    copies = []
    for p in range(parts):
        lax.fori_loop(p * part, (p + 1) * part, fill, 0, unroll=2)
        rows = pl.ds(p * part, part)
        copies.append(pltpu.make_async_copy(late.at[rows], late_hbm.at[rows], sems.at[p]))
        copies[-1].start()
    for copy in copies:
        copy.wait()


def gather_windows(past, block_order, recv):
    blocks = block_order.shape[0]
    shape = lambda size: (blocks, size, past // 4, 16, HEAD)
    early, late = shape(FIRST), shape(2 * KV_HEADS - FIRST)
    return pl.pallas_call(
        functools.partial(gather_kernel, past),
        out_shape=[
            jax.ShapeDtypeStruct(early, jnp.bfloat16),
            jax.ShapeDtypeStruct(late, jnp.bfloat16),
        ],
        in_specs=[
            pl.BlockSpec(memory_space=pltpu.SMEM),
            pl.BlockSpec(memory_space=pltpu.VMEM),
        ],
        out_specs=[
            pl.BlockSpec(memory_space=pltpu.VMEM),
            pl.BlockSpec(memory_space=pltpu.HBM),
        ],
        scratch_shapes=[
            pltpu.SMEM((blocks,), jnp.int32),
            pltpu.VMEM((blocks, KV_HEADS, 8, HEAD), jnp.float32),
            pltpu.VMEM((blocks, KV_HEADS, 8, HEAD), jnp.float32),
            pltpu.VMEM(late, jnp.bfloat16),
            pltpu.SemaphoreType.DMA((4,)),
        ],
        compiler_params=pltpu.CompilerParams(vmem_limit_bytes=24 << 20),
        cost_estimate=pl.CostEstimate(flops=0, bytes_accessed=10 << 20, transcendentals=0),
        name="gather_windows",
    )(block_order, recv)


def mark_documents(lengths_ref, place, keys, stacked):
    total_keys, rows = keys.shape[1], stacked.shape[1] // GROUP
    lane = lax.broadcasted_iota(jnp.int32, (8, HEAD), 1)
    row = lax.broadcasted_iota(jnp.int32, (8, HEAD), 0)
    start = jnp.full((8, HEAD), 1 << 30, jnp.int32)
    end = start
    at = 0
    for d in range(lengths_ref.shape[0]):
        start = jnp.where(lane == d, at, start)
        at += lengths_ref[d]
        end = jnp.where(lane == d, at, end)

    def pair(pos_a, pos_b, inside, outside):
        both = [
            jnp.where((pos >= start) & (pos < end), inside, outside) for pos in (pos_a, pos_b)
        ]
        return jnp.concatenate(both, axis=0).astype(jnp.bfloat16)

    past_keys = total_keys - rows
    slots = past_keys // rows
    origins = []
    for slot in range(0, slots, 2):
        block = place - 1 - slot - row // THIN
        origins.append(jnp.where(block >= 0, block * rows + row % THIN, -(1 << 20)))

    def past(i, carry):
        for tile in range(slots // 4):
            to = pl.ds(pl.multiple_of((i * (slots // 4) + tile) * 16, 16), 16)
            pos = [origins[2 * tile + half] + i * THIN for half in range(2)]
            marks = pair(*pos, 0.0, HIDDEN)
            for slot in range(2):
                keys[slot, to, HEAD:] = marks
        return carry

    lax.fori_loop(0, rows // THIN, past, 0, unroll=16)
    for r in range(0, rows, 16):
        base = place * rows + r + row
        marks = pair(base, base + 8, 0.0, HIDDEN)
        for slot in range(2):
            keys[slot, past_keys + r : past_keys + r + 16, HEAD:] = marks
        marks = pair(base, base + 8, 1.0, 0.0)
        for slot in range(2):
            for g in range(GROUP):
                stacked[slot, g * rows + r : g * rows + r + 16, HEAD:] = marks


def attend_kernel(early, first, units, lengths_ref, order_ref, me_ref, q_hbm, k_hbm, v_hbm, *rest):
    (out_hbm, keys, values, stacked, scores_a, scores_b, peak_a, peak_b) = rest[-19:-11]
    (q_held, k_held, v_held, kw_held, vw_held, out_held) = rest[-11:-5]
    q_sems, own_sems, k_sems, v_sems, out_sems = rest[-5:]
    rows = q_held.shape[1]
    total_keys = keys.shape[1]
    past_keys = total_keys - rows
    tall = STACK * rows
    wide = STACK * HEAD
    stacks = GROUP // STACK
    window = rest[0]

    def columns(c, width, part=0):
        at = (first + c) * GROUP * HEAD + part * wide if width == wide else (first + c) * HEAD
        return pl.ds(pl.multiple_of(at, HEAD), width)

    def q_copy(c, slot, part):
        return pltpu.make_async_copy(
            q_hbm.at[:, columns(c, wide, part)],
            q_held.at[slot, :, pl.ds(part * wide, wide)],
            q_sems.at[slot, part],
        )

    def own_copy(c, slot, i):
        hbm, held = ((k_hbm, k_held), (v_hbm, v_held))[i]
        return pltpu.make_async_copy(
            hbm.at[:, columns(c, HEAD)], held.at[slot], own_sems.at[slot, i]
        )

    def k_copy(c, slot):
        at = 2 * c if early else jnp.maximum(2 * c - 1, 0)
        return pltpu.make_async_copy(window.at[:, at], kw_held.at[slot], k_sems.at[slot])

    def v_copy(c, slot):
        at = 2 * c + 1 if early else 2 * c
        return pltpu.make_async_copy(window.at[:, at], vw_held.at[slot], v_sems.at[slot])

    def out_copy(c, slot, part):
        return pltpu.make_async_copy(
            out_held.at[slot, :, pl.ds(part * wide, wide)],
            out_hbm.at[:, columns(c, wide, part)],
            out_sems.at[slot, part],
        )

    def start_front(c, slot, copy=None):
        (copy or k_copy(c, slot)).start()
        own_copy(c, slot, 0).start()
        for part in range(stacks):
            q_copy(c, slot, part).start()

    def wait_front(c, slot):
        k_copy(c, slot).wait()
        own_copy(c, slot, 0).wait()
        for part in range(stacks):
            q_copy(c, slot, part).wait()

    def start_back(c, slot):
        own_copy(c, slot, 1).start()
        v_copy(c, slot).start()

    begin = None
    if not early:
        begin = pltpu.make_async_copy(rest[1].at[:, FIRST - 1], kw_held.at[0], k_sems.at[0])
    start_front(0, 0, begin)
    start_back(0, 0)
    start_front(1, 1)
    mark_documents(lengths_ref, order_ref[me_ref[0]], keys, stacked)
    values[:, HEAD:] = jnp.ones((total_keys, HEAD), jnp.bfloat16)
    scale = math.log2(math.e) / math.sqrt(HEAD)
    tiles = [(t, t + rows) for t in range(0, total_keys, rows)]
    causal = lax.broadcasted_iota(jnp.int32, (tall, rows), 0) % rows >= lax.broadcasted_iota(
        jnp.int32, (tall, rows), 1
    )

    def score(g, scores, peak, slot):
        q = stacked[slot, g * tall : (g + 1) * tall, :]
        most = None
        for a, b in tiles:
            s = lax.dot_general(
                q, keys[slot, a:b, :], (((1,), (1,)), ((), ())), preferred_element_type=jnp.float32
            )
            if a == past_keys:
                s = jnp.where(causal, s, HIDDEN)
            scores[:, a:b] = s
            for lane in range(0, rows, HEAD):
                part = s[:, lane : lane + HEAD]
                most = part if most is None else jnp.maximum(most, part)
        peak[...] = jnp.broadcast_to(jnp.max(most, axis=1, keepdims=True), (tall, HEAD))

    def mix(g, scores, peak, slot):
        most = jnp.concatenate([peak[...]] * (rows // HEAD), axis=1)
        mixed = None
        for a, b in tiles:
            w = jnp.exp2((scores[:, a:b] - most) * scale).astype(jnp.bfloat16)
            part = jnp.dot(w, values[a:b, :], preferred_element_type=jnp.float32)
            mixed = part if mixed is None else mixed + part
        out = (mixed[:, :HEAD] / mixed[:, HEAD:]).astype(jnp.bfloat16)
        for h in range(STACK):
            at = (g * STACK + h) * HEAD
            out_held[slot, :, at : at + HEAD] = out[h * rows : (h + 1) * rows]

    first_buffer, second_buffer = (scores_a, peak_a), (scores_b, peak_b)

    def build_front(slot):
        keys[slot, :past_keys, :HEAD] = kw_held[slot].reshape(past_keys, HEAD)
        keys[slot, past_keys:, :HEAD] = k_held[slot]
        for g in range(GROUP):
            q = q_held[slot, :, g * HEAD : (g + 1) * HEAD]
            stacked[slot, g * rows : (g + 1) * rows, :HEAD] = q

    def build_back(slot):
        values[:past_keys, :HEAD] = vw_held[slot].reshape(past_keys, HEAD)
        values[past_keys:, :HEAD] = v_held[slot]

    def wait_back(c, slot):
        own_copy(c, slot, 1).wait()
        v_copy(c, slot).wait()

    def wait_out(c, slot):
        for part in range(stacks):
            out_copy(c, slot, part).wait()

    def start_out(c, slot):
        for part in range(stacks):
            out_copy(c, slot, part).start()

    def one_head(c, carry):
        slot = lax.rem(c, 2)
        other = 1 - slot
        wait_back(c, slot)
        wait_front(c + 1, other)
        pl.when(c + 2 < units)(lambda: start_front(c + 2, slot))
        start_back(c + 1, other)
        pl.when(c >= 2)(lambda: wait_out(c - 2, slot))
        build_back(slot)
        build_front(other)
        score(1, *second_buffer, slot)
        mix(0, *first_buffer, slot)
        score(0, *first_buffer, other)
        mix(1, *second_buffer, slot)
        start_out(c, slot)
        return carry

    wait_front(0, 0)
    build_front(0)
    score(0, *first_buffer, 0)
    lax.fori_loop(0, units - 1, one_head, 0)
    c = units - 1
    slot = c % 2
    wait_back(c, slot)
    if c >= 2:
        wait_out(c - 2, slot)
    build_back(slot)
    score(1, *second_buffer, slot)
    mix(0, *first_buffer, slot)
    mix(1, *second_buffer, slot)
    start_out(c, slot)
    wait_out(c - 1, 1 - slot)
    wait_out(c, slot)


def attend(lengths, order, me, queries, own_keys, own_values, windows, attended):
    rows, width = queries.shape
    early = attended is None
    first = 0 if early else FIRST // 2
    units = FIRST // 2 if early else KV_HEADS - first
    sources, _, tiles = windows[0].shape[:3]
    total_keys = sources * tiles * 16 + rows
    tall = STACK * rows
    smem, hbm = pl.BlockSpec(memory_space=pltpu.SMEM), pl.BlockSpec(memory_space=pl.ANY)
    operands = [lengths, order, me, queries, own_keys, own_values]
    operands += [windows[0]] if early else [windows[1], windows[0], attended]
    held = lambda *shape: pltpu.VMEM((2, *shape), jnp.bfloat16)
    done = units * GROUP * rows * total_keys
    return pl.pallas_call(
        functools.partial(attend_kernel, early, first, units),
        out_shape=jax.ShapeDtypeStruct((rows, width), jnp.bfloat16),
        in_specs=[smem] * 3 + [hbm] * (len(operands) - 3),
        out_specs=hbm,
        scratch_shapes=[
            held(total_keys, 2 * HEAD),
            pltpu.VMEM((total_keys, 2 * HEAD), jnp.bfloat16),
            held(GROUP * rows, 2 * HEAD),
            pltpu.VMEM((tall, total_keys), jnp.float32),
            pltpu.VMEM((tall, total_keys), jnp.float32),
            pltpu.VMEM((tall, HEAD), jnp.float32),
            pltpu.VMEM((tall, HEAD), jnp.float32),
            held(rows, GROUP * HEAD),
            held(rows, HEAD),
            held(rows, HEAD),
            held(sources, tiles, 16, HEAD),
            held(sources, tiles, 16, HEAD),
            held(rows, GROUP * HEAD),
            pltpu.SemaphoreType.DMA((2, GROUP // STACK)),
            pltpu.SemaphoreType.DMA((2, 2)),
            pltpu.SemaphoreType.DMA((2,)),
            pltpu.SemaphoreType.DMA((2,)),
            pltpu.SemaphoreType.DMA((2, GROUP // STACK)),
        ],
        input_output_aliases={} if early else {len(operands) - 1: 0},
        compiler_params=pltpu.CompilerParams(vmem_limit_bytes=VMEM),
        cost_estimate=pl.CostEstimate(
            flops=done * 2 * 4 * HEAD, bytes_accessed=units << 21, transcendentals=done
        ),
        name="attend",
    )(*operands)


def body(queries, rotated_key_rows, stored_value_rows, doc_lengths, block_order):
    axes = ("context", "tensor")
    past = 8
    me = lax.axis_index("context") * lax.axis_size("tensor") + lax.axis_index("tensor")
    me = me.astype(jnp.int32).reshape(1)
    pieces = cut_pieces(rotated_key_rows, stored_value_rows)
    pieces, me = lax.optimization_barrier((pieces, me))
    recv = lax.all_to_all(pieces, axes, split_axis=0, concat_axis=0, tiled=True)
    sends = gather_windows(past, block_order, recv)
    sends, me = lax.optimization_barrier((sends, me))
    window = lax.all_to_all(sends[0], axes, split_axis=0, concat_axis=0, tiled=True)
    window, me, send = lax.optimization_barrier((window, me, sends[1]))
    late = lax.all_to_all(send, axes, split_axis=0, concat_axis=0, tiled=True)
    own = (queries, rotated_key_rows, stored_value_rows)
    attended = attend(doc_lengths, block_order, me, *own, (window,), None)
    return attend(doc_lengths, block_order, me, *own, (window, late), attended)


def solution(mesh):
    rows = P(("dp", "context", "tensor"), None)
    return jax.shard_map(
        body,
        mesh=mesh,
        in_specs=(rows, rows, rows, P("dp"), P("dp")),
        out_specs=rows,
        check_vma=False,
    )
```
